32 devices in a mesh: groups: 2 (over y), slab: 4 (over z), chan: 4 (over x, core).
Axes of the slice: x: 2, y: 2, z: 4, core: 2. Of those that a mesh axis runs over, the one named last changes fastest.
Arguments:
- features: bfloat16 [96, 8192], P('chan', ('groups', 'slab')), parts along dimension 1, may hold values from -6 to 6
- neighbors: int32 [27, 8192], P(None, ('groups', 'slab')), parts along dimension 1, may hold values from 0 to 1536, as said below
- halo_rows: int32 [2, 2048], P(None, ('groups', 'slab')), parts along dimension 1, may hold values from 0 to 1023
- counts: int32 [8], P(('groups', 'slab')), parts along dimension 0, may hold values from 512 to 1024, as said below
- owners: int32 [8192, 1], P(('groups', 'slab')), parts along dimension 0, may hold values from 0 to 3; in each aligned block of 1024 rows (0 to 1023, 1024 to 2047, ...) at most 288 rows name the same one
- children: int32 [8, 4608], P(None, ('groups', 'slab')), parts along dimension 1, may hold values from 0 to 1152, as said below
- weight_fine: bfloat16 [27, 96, 96], replicated, may hold values from -0.15625 to 0.15625
- weight_coarse: bfloat16 [8, 192, 96], replicated, may hold values from -0.625 to 0.625
- cotangent: bfloat16 [192, 4608], P('chan', ('groups', 'slab')), parts along dimension 1, may hold values from -6 to 6
Outputs:
- coarse: bfloat16 [192, 4608], P('chan', ('groups', 'slab')), parts along dimension 1
- grad_fine: float32 [54, 96, 96], P('groups', 'chan'), parts along dimension 0
- grad_coarse: float32 [16, 192, 96], P('groups', 'chan'), parts along dimension 0
- grad_input: bfloat16 [96, 8192], P('chan', ('groups', 'slab')), parts along dimension 1
The draws below stay inside these ranges and needn't reach their ends.
There are 2 independent parts, one for each index of `groups`. The reference program is written for one: setup_inputs(seed, part) draws one part's arguments, and reference() takes and returns one part's arrays. A program takes and returns all parts, laid end to end along the dimension named above; an argument that names none is the same for every part. Nothing has to cross between parts.
Inputs may be any that keep to these rules, and one draw needn't show every extreme that they name: `neighbors`: for each tile and offset, the entries below 1536 are distinct; 1536 marks a missing neighbour; offset 27 // 2 maps every row to itself. `counts`: some tile is full. `owners`: the rows of one tile name each owner at most 288 times, a bound that some block reaches. `children`: for each tile, the entries below 1152 are distinct over all offsets and coarse rows; 1152 marks a missing child.
All inputs are finite; a program needn't handle non-finite values.
Results may differ from the reference program's by a relative error of at most 0.005.
Values may be sent and summed in bfloat16 or wider, within the bound.
No kernel may reach another device: no remote copies, remote signals or barrier semaphores. Data moves between devices by JAX's collectives and lax.ppermute only.
A program may use at most 64 MiB of HBM per device.

```python
import math
import jax
import jax.numpy as jnp
import numpy as np
from jax import lax

C1 = 96
C2 = 192
K = 27
CH = 8
R_DEV = 1024
TILES = 4
HALO = 256
CAP = 288
NC = 1152
CR = 576
ROWS = 4096
HROWS = 1024
CROWS = 2304


def draw_neighbors(key, part):
    key = jax.random.fold_in(key, 11)
    ext_rows = R_DEV + 2 * HALO
    keys = jax.random.split(key, K * TILES)

    def one_offset(subkey):
        first, second = jax.random.split(subkey)
        order = jax.random.permutation(first, ext_rows)[:R_DEV]
        keep = jax.random.randint(second, (R_DEV,), 0, 20) < 11
        return jnp.where(keep, order, ext_rows).astype(jnp.int32)
    table = jax.vmap(one_offset)(keys).reshape(K, TILES, R_DEV)
    centre = jnp.broadcast_to(jnp.arange(R_DEV, dtype=jnp.int32), (TILES, R_DEV))
    table = table.at[K // 2].set(centre)
    return table.reshape(K, TILES * R_DEV)


def draw_children(key, part):
    key = jax.random.fold_in(key, 12)
    keys = jax.random.split(key, TILES)

    def one_tile(subkey):
        order = jax.random.permutation(subkey, CH * CR)
        return jnp.where(order < NC, order, NC).astype(jnp.int32).reshape(CH, CR)
    table = jax.vmap(one_tile)(keys)
    return table.transpose(1, 0, 2).reshape(CH, TILES * CR)


def draw_counts(key, part):
    key = jax.random.fold_in(key, 13)
    first, second = jax.random.split(key)
    drawn = jax.random.randint(first, (TILES,), R_DEV // 2, R_DEV + 1)
    full_tile = jax.random.randint(second, (), 0, TILES)
    return jnp.where(jnp.arange(TILES) == full_tile, R_DEV, drawn).astype(jnp.int32)


def place_ends(values, stream_key, low, largest):
    longest = values.shape.index(max(values.shape))
    spots = []
    for shift in (0, 1):
        where = [jax.random.randint(jax.random.fold_in(stream_key, axis), (), 0, length) for axis, length in enumerate(values.shape)]
        where[longest] = (where[longest] + shift) % values.shape[longest]
        spots.append(tuple(where))
    return values.at[spots[0]].set(low).at[spots[1]].set(largest)


def block_levels(stream_key, extent, pieces, low, high):
    gain = 1.0
    for position, parts in pieces:
        draws = jax.random.uniform(jax.random.fold_in(jax.random.fold_in(stream_key, 6), position), (parts,), jnp.float32, low / len(pieces), high / len(pieces))
        gain = gain * jnp.repeat(jnp.exp(draws), extent[position] // parts).reshape((-1,) + (1,) * (len(extent) - 1 - position))
    return gain


def shared_out(rng, own, number, rows, amount, top, bound, skew):
    sequence = jax.random.permutation(rng, amount)
    packed, ordinary = shares(amount, rows * top, bound, skew, True), shares(amount, rows * top, bound, skew, False)
    places = jnp.arange(amount)

    def named(sizes, offset_by):
        used = int((sizes > 0).sum())
        fixed = max(1, used // 4)
        passed = fixed + (places - fixed + offset_by * (used - fixed)) % max(1, amount - fixed)
        return jnp.zeros((amount,), jnp.int32).at[sequence[jnp.where(places < fixed, places, passed)]].set(jnp.asarray(sizes, jnp.int32))

    sizes = jnp.where(number % 4 == 0, named(packed, number // 4), named(ordinary, number - number // 4 - 1))
    mixed = jax.random.permutation(jax.random.fold_in(own, 3), amount)
    source_of, taker = mixed[0:amount // 2 * 2:2], mixed[1:amount // 2 * 2:2]
    margin = jnp.minimum(sizes[source_of] - 1, bound - sizes[taker]) // 2
    margin = jnp.where((source_of == sequence[0]) | (taker == sequence[0]) | (sizes[taker] == 0), 0, jnp.maximum(margin, 0))
    passed = jax.random.randint(jax.random.fold_in(own, 4), (amount // 2,), 0, 1 << 20) % (margin + 1)
    sizes = sizes.at[source_of].add(-passed).at[taker].add(passed)
    items = jnp.searchsorted(jnp.cumsum(sizes), jnp.arange(rows * top), side="right").astype(jnp.int32)
    grid = items.reshape(top, rows).T
    grid = grid[jax.random.permutation(jax.random.fold_in(own, 1), rows)]
    offset_by = jax.random.randint(jax.random.fold_in(own, 2), (rows, 1), 0, top)
    return jnp.take_along_axis(grid, (jnp.arange(top)[None, :] + offset_by) % top, axis=1)


def shares(number_of, total, most, slope, full):
    portions = [(1 << 20) // math.isqrt(rank ** slope) + 1 for rank in range(1, number_of + 1)]
    largest = most if full else min(most, max(-(-total // number_of), total * portions[0] // sum(portions)))
    least = 1 if total - largest >= number_of - 1 else 0
    given, surplus = [largest] + [least] * (number_of - 1), total - largest - least * (number_of - 1)
    while surplus > 0:
        movable = [i for i in range(1, number_of) if given[i] < largest] or [i for i in range(1, number_of) if given[i] < most]
        whole, remaining = sum([portions[i] for i in movable]), surplus
        for i in movable:
            addition = min(most - given[i], max(1, remaining * portions[i] // whole), surplus)
            given[i] = given[i] + addition
            surplus = surplus - addition
    return np.array(given)


def noise(rng, shape, width, limit, pieces=(), kind=jnp.bfloat16):
    factor_of = block_levels(rng, shape, pieces, -0.22, 0.18) if pieces else 1.0
    values = jax.random.normal(rng, shape, jnp.float32) * width * factor_of
    return jnp.minimum(jnp.maximum(values, -limit), limit).astype(kind)


def setup_inputs(seed: int = 0, part: int = 0) -> dict:
    key_list = jax.random.split(jax.random.key(seed), 10)
    part_keys = jax.random.split(jax.random.fold_in(key_list[9], part), 10)
    features = noise(part_keys[0], (C1, ROWS), 1.0, 6.0, ((0, 4), (1, 4)))
    neighbors = draw_neighbors(jax.random.fold_in(jax.random.fold_in(key_list[9], part), 71), part)
    halo_rows = place_ends(jax.random.randint(part_keys[2], (2, HROWS), 0, R_DEV), jax.random.fold_in(part_keys[2], 1), 0, R_DEV - 1).astype(jnp.int32)
    counts = draw_counts(jax.random.fold_in(jax.random.fold_in(key_list[9], part), 71), part)
    owners_keys = jax.random.split(jax.random.fold_in(part_keys[4], 1), ROWS // R_DEV)
    owners_turns = jax.random.permutation(jax.random.fold_in(part_keys[4], 3), ROWS // R_DEV)
    owners = jax.vmap(lambda own, number: shared_out(jax.random.fold_in(part_keys[4], 2), own, number, R_DEV, TILES, 1, CAP, 1))(owners_keys, owners_turns).reshape((ROWS, 1))
    children = draw_children(jax.random.fold_in(jax.random.fold_in(key_list[9], part), 71), part)
    weight_fine = noise(key_list[6], (K, C1, C1), (K * C1 // 2) ** -0.5, 0.15625)
    weight_coarse = noise(key_list[7], (CH, C2, C1), C1 ** -0.5, 0.625)
    cotangent = noise(part_keys[8], (C2, CROWS), 1.0, 6.0, ((0, 4), (1, 4)))
    return {"features": features, "neighbors": neighbors, "halo_rows": halo_rows, "counts": counts, "owners": owners, "children": children, "weight_fine": weight_fine, "weight_coarse": weight_coarse, "cotangent": cotangent}


def by_tile(flat):
    channels = flat.shape[0]
    return flat.reshape(channels, TILES, -1).transpose(1, 0, 2)


def from_tiles(tiled):
    return tiled.transpose(1, 0, 2).reshape(tiled.shape[1], -1)


def pick_columns(block, indices):
    return block[:, indices]


def reference(features, neighbors, halo_rows, counts, owners, children, weight_fine, weight_coarse, cotangent):
    ext_rows = R_DEV + 2 * HALO
    row_valid = (jnp.arange(R_DEV)[None, :] < counts[:, None]).astype(jnp.float32)
    fine_feat = (by_tile(features).astype(jnp.float32) * row_valid[:, None, :]).astype(jnp.bfloat16)
    neighbor_tiles = neighbors.reshape(K, TILES, R_DEV).transpose(1, 0, 2)
    halo_tiles = halo_rows.reshape(2, TILES, HALO).transpose(1, 0, 2)
    lower_list = jax.vmap(pick_columns)(fine_feat, halo_tiles[:, 0])
    upper_list = jax.vmap(pick_columns)(fine_feat, halo_tiles[:, 1])
    empty_rim = jnp.zeros((1, C1, HALO), jnp.bfloat16)
    from_below = jnp.concatenate([empty_rim, upper_list[:-1]], axis=0)
    from_above = jnp.concatenate([lower_list[1:], empty_rim], axis=0)
    ext_table = jnp.concatenate([fine_feat, from_below, from_above, jnp.zeros((TILES, C1, 1), jnp.bfloat16)], axis=2)

    def fine_conv(step_input):
        table_tile, neighbor_tile = step_input

        def offset_step(running, offset_input):
            weight_slice, indices = offset_input
            return running + jnp.dot(weight_slice, table_tile[:, indices], preferred_element_type=jnp.float32), None

        return lax.scan(offset_step, jnp.zeros((C1, R_DEV), jnp.float32), (weight_fine, neighbor_tile))[0]

    pre_act = lax.map(fine_conv, (ext_table, neighbor_tiles))
    hidden = (jnp.maximum(pre_act, 0.0) * row_valid[:, None, :]).astype(jnp.bfloat16)
    dest_tile = owners.reshape(TILES, R_DEV).astype(jnp.int32)
    one_hot = (dest_tile[:, :, None] == jnp.arange(TILES, dtype=jnp.int32)[None, None, :]).astype(jnp.int32)
    slot_rank = jnp.sum(jnp.cumsum(one_hot, axis=1) * one_hot, axis=2) - 1
    slot_index = (dest_tile * CAP + slot_rank).astype(jnp.int32)

    def place_rows(block, indices):
        return jnp.zeros((C1, NC), jnp.bfloat16).at[:, indices].set(block)

    outgoing = jax.vmap(place_rows)(hidden, slot_index)
    incoming = outgoing.reshape(TILES, C1, TILES, CAP).transpose(2, 1, 0, 3).reshape(TILES, C1, NC)
    padded = jnp.concatenate([incoming, jnp.zeros((TILES, C1, 1), jnp.bfloat16)], axis=2)
    child_tiles = children.reshape(CH, TILES, CR).transpose(1, 0, 2)

    def coarse_conv(step_input):
        slots_tile, child_tile = step_input

        def child_step(running, child_input):
            weight_slice, indices = child_input
            return running + jnp.dot(weight_slice, slots_tile[:, indices], preferred_element_type=jnp.float32), None

        return lax.scan(child_step, jnp.zeros((C2, CR), jnp.float32), (weight_coarse, child_tile))[0]

    coarse_acc = lax.map(coarse_conv, (padded, child_tiles))
    coarse = from_tiles(coarse_acc.astype(jnp.bfloat16))
    grad_scale = float(ROWS) ** -0.5
    grad_tiles = by_tile(cotangent)

    def coarse_back(step_input):
        slots_tile, child_tile, grad_tile = step_input

        def child_step(running, child_input):
            weight_slice, indices = child_input
            grad_term = jnp.dot(grad_tile, slots_tile[:, indices].T, preferred_element_type=jnp.float32)
            running = running.at[:, indices].set(jnp.dot(weight_slice.T, grad_tile, preferred_element_type=jnp.float32))
            return running, grad_term

        running, grad_term = lax.scan(child_step, jnp.zeros((C1, NC + 1), jnp.float32), (weight_coarse, child_tile))
        return running[:, :NC], grad_term

    slot_grads, coarse_terms = lax.map(coarse_back, (padded, child_tiles, grad_tiles))
    grad_coarse = jnp.sum(coarse_terms, axis=0) * grad_scale
    slot_grads = slot_grads.astype(jnp.bfloat16)
    returned = slot_grads.reshape(TILES, C1, TILES, CAP).transpose(2, 1, 0, 3).reshape(TILES, C1, NC)
    grad_hidden = jax.vmap(pick_columns)(returned, slot_index)
    grad_pre = (grad_hidden.astype(jnp.float32) * jnp.where(pre_act > 0, row_valid[:, None, :], 0.0)).astype(jnp.bfloat16)

    def fine_back(step_input):
        table_tile, neighbor_tile, grad_tile = step_input

        def offset_step(running, offset_input):
            weight_slice, indices = offset_input
            grad_term = jnp.dot(grad_tile, table_tile[:, indices].T, preferred_element_type=jnp.float32)
            running = running.at[:, indices].add(jnp.dot(weight_slice.T, grad_tile, preferred_element_type=jnp.float32))
            return running, grad_term

        running, grad_term = lax.scan(offset_step, jnp.zeros((C1, ext_rows + 1), jnp.float32), (weight_fine, neighbor_tile))
        return running[:, :ext_rows], grad_term

    grad_table, fine_terms = lax.map(fine_back, (ext_table, neighbor_tiles, grad_pre))
    grad_fine = jnp.sum(fine_terms, axis=0) * grad_scale
    zero_rim = jnp.zeros((1, C1, HALO), jnp.float32)
    above_grad = jnp.concatenate([grad_table[1:, :, R_DEV:R_DEV + HALO], zero_rim], axis=0)
    below_grad = jnp.concatenate([zero_rim, grad_table[:-1, :, R_DEV + HALO:]], axis=0)

    def add_rims(own_part, below_part, above_part, low_list, high_list):
        return own_part.at[:, high_list].add(above_part).at[:, low_list].add(below_part)

    grad_rows = jax.vmap(add_rims)(grad_table[:, :, :R_DEV], below_grad, above_grad, halo_tiles[:, 0], halo_tiles[:, 1])
    grad_input = from_tiles((grad_rows * row_valid[:, None, :]).astype(jnp.bfloat16))
    return coarse, grad_fine, grad_coarse, grad_input
```

```python
import functools

import jax
import jax.numpy as jnp
from jax import lax
from jax.experimental import pallas as pl
from jax.experimental.pallas import tpu as pltpu
from jax.sharding import PartitionSpec as P

BF = jnp.bfloat16
F32 = jnp.float32
LO = 256
VMEM_LIMIT = 48 * 1024 * 1024


def up_to(value, step):
    return -(-value // step) * step


def dot(left, right):
    return jnp.dot(left, right, preferred_element_type=F32)


def dot_nt(left, right):
    return lax.dot_general(left, right, (((1,), (1,)), ((), ())), preferred_element_type=F32)


def dot_tn(left, right):
    return lax.dot_general(left, right, (((0,), (0,)), ((), ())), preferred_element_type=F32)


def one_hot(code, width=LO):
    low = code & (width - 1)
    rows = lax.broadcasted_iota(jnp.int32, (width, code.shape[1]), 0)
    return jnp.where(rows == low, 1.0, 0.0).astype(BF)


def gather_columns(blocks, code, channels):
    count = blocks.shape[0] // channels
    high = code >> 8
    found = dot(blocks, one_hot(code))
    picked = jnp.zeros((channels, code.shape[1]), F32)
    for block in range(count):
        picked = jnp.where(high == block, found[block * channels : (block + 1) * channels], picked)
    return picked.astype(BF)


def scatter_columns(values, code, count):
    high = code >> 8
    spread = jnp.concatenate(
        [values * jnp.where(high == block, 1.0, 0.0).astype(BF) for block in range(count)], axis=0
    )
    return dot_nt(spread, one_hot(code))


def split_slot(slots, cap, tiles):
    source = jnp.zeros_like(slots)
    for tile in range(1, tiles + 1):
        source = source + jnp.where(slots >= tile * cap, 1, 0)
    return source, slots - source * cap


def wrapped(value, tiles):
    return jnp.where(value < 0, value + tiles, value)


def own_rows(padded, full, cw, chan):
    line = lax.broadcasted_iota(jnp.int32, (padded, full), 0)
    column = lax.broadcasted_iota(jnp.int32, (padded, full), 1)
    return jnp.where((column == chan * cw + line) & (line < cw), 1.0, 0.0).astype(BF)


def edge_kernel(count_ref, feat_ref, halo_ref, low_ref, high_ref):
    rows = feat_ref.shape[1]
    width = halo_ref.shape[1]
    valid = jnp.where(lax.broadcasted_iota(jnp.int32, (1, rows), 1) < count_ref[0], 1.0, 0.0)
    table = (feat_ref[...].astype(F32) * valid).astype(BF)
    for side, out in ((0, low_ref), (1, high_ref)):
        picks = lax.broadcasted_iota(jnp.int32, (rows, width), 0) == halo_ref[side : side + 1, :]
        out[...] = dot(table, jnp.where(picks, 1.0, 0.0).astype(BF)).astype(BF)


def slot_kernel(tiles, cap, capp, cw, place_ref, cot_ref, child_ref, wc_ref, wf_ref, owner_ref, *rest):
    outs = rest[:tiles]
    slots_ref, wz_ref, cot_pad, code_pad, total = rest[tiles:]
    tile, chan = place_ref[0], place_ref[1]
    kids, width = child_ref.shape
    full = wc_ref.shape[2]
    blocks = tiles * capp // LO
    cot_pad[...] = jnp.zeros_like(cot_pad)
    cot_pad[:, :width] = cot_ref[...]
    source, rank = split_slot(child_ref[...], cap, tiles)
    code = wrapped(source - tile, tiles) * capp + rank
    code_pad[...] = jnp.full(code_pad.shape, tiles * capp, jnp.int32)
    code_pad[:, :width] = jnp.where(source == tiles, tiles * capp, code)
    total[...] = jnp.zeros_like(total)

    @pl.loop(0, kids)
    def _(kid):
        value = dot_tn(wc_ref[kid], cot_pad[...]).astype(BF)
        total[...] += scatter_columns(value, code_pad[pl.ds(kid, 1), :], blocks)

    table = jnp.concatenate(
        [total[block * full : (block + 1) * full, :] for block in range(blocks)], axis=1
    ).astype(BF)
    for step in range(tiles):
        outs[step][...] = table[:, step * capp : (step + 1) * capp]

    owner = owner_ref[...]
    rows = owner.shape[1]
    names = up_to(tiles, 16)
    same = lax.broadcasted_iota(jnp.int32, (names, rows), 0) == owner
    before = lax.broadcasted_iota(jnp.int32, (rows, rows), 0) < lax.broadcasted_iota(
        jnp.int32, (rows, rows), 1
    )
    earlier = dot(jnp.where(same, 1.0, 0.0).astype(BF), jnp.where(before, 1.0, 0.0).astype(BF))
    place = jnp.sum(jnp.where(same, earlier, 0.0), axis=0, keepdims=True).astype(jnp.int32)
    slots_ref[0:1, :] = wrapped(owner - tile, tiles) * capp + place
    slots_ref[1:2, :] = wrapped(tile - owner, tiles) * capp + place

    own = own_rows(wz_ref.shape[1], wf_ref.shape[2], cw, chan)

    @pl.loop(0, wf_ref.shape[0])
    def _(offset):
        wz_ref[offset] = dot_nt(own, wf_ref[offset]).astype(BF)


def forward_kernel(
    tiles, capp, count_ref, feat_ref, below_ref, above_ref, nb_ref, wf_ref, slots_ref, *rest
):
    outs = rest[:tiles]
    gate_ref, picked_ref, blocks_ref, total = rest[tiles:]
    full, rows = feat_ref.shape
    halo = below_ref.shape[1]
    valid = jnp.where(lax.broadcasted_iota(jnp.int32, (1, rows), 1) < count_ref[0], 1.0, 0.0)
    table = jnp.concatenate(
        [(feat_ref[...].astype(F32) * valid).astype(BF), below_ref[...], above_ref[...]], axis=1
    )
    for block in range((rows + 2 * halo) // LO):
        blocks_ref[block * full : (block + 1) * full, :] = table[:, block * LO : (block + 1) * LO]
    total[...] = jnp.zeros_like(total)

    @pl.loop(0, nb_ref.shape[0])
    def _(offset):
        picked = gather_columns(blocks_ref[...], nb_ref[pl.ds(offset, 1), :], full)
        picked_ref[offset] = picked
        total[...] += dot(wf_ref[offset], picked)

    pre = total[...]
    gate_ref[...] = jnp.where(pre > 0, valid, 0.0).astype(BF)
    hidden = (jnp.maximum(pre, 0.0) * valid).astype(BF)
    count = tiles * capp // LO
    placed = scatter_columns(hidden, slots_ref[0:1, :], count).astype(BF)
    outgoing = jnp.concatenate(
        [placed[block * full : (block + 1) * full, :] for block in range(count)], axis=1
    )
    for step in range(tiles):
        outs[step][...] = outgoing[:, step * capp : (step + 1) * capp]


def backward_kernel(tiles, cw, place_ref, slots_ref, gate_ref, picked_ref, nb_ref, wz_ref, *rest):
    takes, rest = rest[:tiles], rest[tiles:]
    outs, rest = rest[:tiles], rest[tiles:]
    own_ref, below_ref, above_ref, blocks_ref, grad_ref, terms, total = rest
    tile, chan = place_ref[0], place_ref[1]
    full, rows = gate_ref.shape
    offsets = nb_ref.shape[0]
    part = outs[0].shape[0]
    padded = wz_ref.shape[1]
    table = jnp.concatenate([take[...] for take in takes], axis=1)
    for block in range(table.shape[1] // LO):
        blocks_ref[block * full : (block + 1) * full, :] = table[:, block * LO : (block + 1) * LO]
    grad = gather_columns(blocks_ref[...], slots_ref[1:2, :], full) * gate_ref[...]
    grad_ref[...] = grad
    own_grad = dot(own_rows(padded, full, cw, chan), grad).astype(BF)
    total[...] = jnp.zeros_like(total)
    terms[...] = jnp.zeros_like(terms)
    count = total.shape[0] // padded

    @pl.loop(0, offsets)
    def _(offset):
        terms[offset] = dot_nt(own_grad, picked_ref[offset])
        value = dot(wz_ref[offset], grad_ref[...]).astype(BF)
        total[...] += scatter_columns(value, nb_ref[pl.ds(offset, 1), :], count)

    for step in range(tiles):
        peer = lax.rem(tile + step, tiles)
        outs[step][...] = terms[pl.ds(peer * part, part), :cw, :].astype(BF)
    for block in range(rows // LO):
        own_ref[:, block * LO : (block + 1) * LO] = total[block * padded : block * padded + cw, :]
    halo = below_ref.shape[1]
    for start, out in ((rows, below_ref), (rows + halo, above_ref)):
        for piece in range(halo // LO):
            block = start // LO + piece
            out[:, piece * LO : (piece + 1) * LO] = total[
                block * padded : block * padded + cw, :
            ].astype(BF)


def coarse_kernel(tiles, cap, capp, place_ref, child_ref, wc_ref, cot_ref, *rest):
    takes, rest = rest[:tiles], rest[tiles:]
    coarse_ref, rest = rest[0], rest[1:]
    outs, rest = rest[:tiles], rest[tiles:]
    blocks_ref, code_pad, cot_pad, total, terms = rest
    tile, chan = place_ref[0], place_ref[1]
    kids, width = child_ref.shape
    full = wc_ref.shape[2]
    own = cot_ref.shape[0]
    part = outs[0].shape[0]
    cot_pad[...] = jnp.zeros_like(cot_pad)
    cot_pad[:, :width] = cot_ref[...]
    source, rank = split_slot(child_ref[...], cap, tiles)
    code = wrapped(tile - source, tiles) * capp + rank
    code_pad[...] = jnp.full(code_pad.shape, tiles * capp, jnp.int32)
    code_pad[:, :width] = jnp.where(source == tiles, tiles * capp, code)
    table = jnp.concatenate([take[...] for take in takes], axis=1)
    for block in range(table.shape[1] // LO):
        blocks_ref[block * full : (block + 1) * full, :] = table[:, block * LO : (block + 1) * LO]
    total[...] = jnp.zeros_like(total)
    terms[...] = jnp.zeros_like(terms)

    @pl.loop(0, kids)
    def _(kid):
        picked = gather_columns(blocks_ref[...], code_pad[pl.ds(kid, 1), :], full)
        total[...] += dot(wc_ref[kid], picked)
        terms[kid] = dot_nt(cot_pad[...], picked)

    coarse_ref[...] = total[pl.ds(pl.multiple_of(chan * own, 8), own), :][:, :width].astype(BF)
    for step in range(tiles):
        peer = lax.rem(tile + step, tiles)
        outs[step][...] = terms[pl.ds(peer * part, part)].astype(BF)


def finish_kernel(count_ref, own_ref, halo_ref, above_ref, below_ref, out_ref):
    rows = own_ref.shape[1]
    width = halo_ref.shape[0]
    valid = jnp.where(lax.broadcasted_iota(jnp.int32, (1, rows), 1) < count_ref[0], 1.0, 0.0)
    total = own_ref[...]
    for side, take in ((1, above_ref), (0, below_ref)):
        picks = lax.broadcasted_iota(jnp.int32, (width, rows), 1)
        hits = jnp.where(picks == halo_ref[:, side : side + 1], 1.0, 0.0).astype(BF)
        total = total + dot(take[...], hits)
    out_ref[...] = (total * valid).astype(BF)


def sum_kernel(tiles, scale, *refs):
    for half in range(2):
        takes, out = refs[half * tiles : (half + 1) * tiles], refs[2 * tiles + half]
        total = takes[0][...].astype(F32)
        for take in takes[1:]:
            total = total + take[...].astype(F32)
        out[...] = (total * scale).astype(BF)


def collect_kernel(tiles, place_ref, *refs):
    tile = place_ref[0]
    for half in range(2):
        takes, out = refs[half * tiles : (half + 1) * tiles], refs[2 * tiles + half]
        part = takes[0].shape[0]
        for step in range(tiles):
            peer = lax.rem(tile + tiles - step, tiles)
            for line in range(part):
                index = peer * part + line

                @pl.when(index < out.shape[0])
                def _(index=index, line=line, take=takes[step], out=out):
                    out[index] = take[line].astype(F32)


def call(body, outs, scalars, arrays, scratch=()):
    return pl.pallas_call(
        body,
        out_shape=outs,
        in_specs=[pl.BlockSpec(memory_space=pltpu.SMEM)] * scalars
        + [pl.BlockSpec(memory_space=pltpu.VMEM)] * (len(arrays) - scalars),
        out_specs=jax.tree.map(lambda _: pl.BlockSpec(memory_space=pltpu.VMEM), outs),
        scratch_shapes=scratch,
        compiler_params=pltpu.CompilerParams(vmem_limit_bytes=VMEM_LIMIT),
    )(*arrays)


def exchange(chunks):
    tiles = len(chunks)
    if tiles <= 4:
        return [chunks[0]] + [
            lax.ppermute(chunks[step], "slab", [(i, (i + step) % tiles) for i in range(tiles)])
            for step in range(1, tiles)
        ]
    tile = lax.axis_index("slab")
    order = jnp.arange(tiles)
    stacked = jnp.take(jnp.stack(chunks), (order - tile) % tiles, axis=0)
    taken = lax.all_to_all(stacked, "slab", split_axis=0, concat_axis=0, tiled=True)
    taken = jnp.take(taken, (tile - order) % tiles, axis=0)
    return [taken[step] for step in range(tiles)]


def spread(chunk, tiles):
    return exchange([chunk] * tiles)


def local(
    features, neighbors, halo_rows, counts, owners, children, weight_fine, weight_coarse, cotangent
):
    tiles = lax.axis_size("slab")
    tile, chan = lax.axis_index("slab"), lax.axis_index("chan")
    cw, rows = features.shape
    halo = halo_rows.shape[1]
    own, width = cotangent.shape
    offsets, full = weight_fine.shape[0], weight_fine.shape[2]
    kids, wide = weight_coarse.shape[0], weight_coarse.shape[1]
    cap = 9 * rows // (8 * tiles)
    capp = up_to(cap, 128)
    padded = up_to(cw, 16)
    widep = up_to(width, 128)
    blocks = tiles * capp // LO
    fine_part, coarse_part = -(-offsets // tiles), -(-kids // tiles)
    shape = jax.ShapeDtypeStruct
    place = jnp.stack([tile, chan]).astype(jnp.int32)

    feat = lax.all_gather(features, "chan", axis=0, tiled=True)
    cot = lax.all_gather(cotangent, "chan", axis=0, tiled=True)
    low, high = call(
        edge_kernel, [shape((full, halo), BF)] * 2, 1, (counts, feat, halo_rows)
    )
    up = [(i, i + 1) for i in range(tiles - 1)]
    down = [(i + 1, i) for i in range(tiles - 1)]
    below = lax.ppermute(high, "slab", up)
    above = lax.ppermute(low, "slab", down)

    *slot_out, slots, wz = call(
        functools.partial(slot_kernel, tiles, cap, capp, cw),
        [shape((full, capp), BF)] * tiles
        + [shape((8, rows), jnp.int32), shape((offsets, padded, full), BF)],
        1,
        (place, cot, children, weight_coarse, weight_fine, owners.reshape(1, rows)),
        [
            pltpu.VMEM((wide, widep), BF),
            pltpu.VMEM((kids, widep), jnp.int32),
            pltpu.VMEM((blocks * full, LO), F32),
        ],
    )
    slot_in = exchange(slot_out)

    *hidden_out, gate, picked = call(
        functools.partial(forward_kernel, tiles, capp),
        [shape((full, capp), BF)] * tiles
        + [shape((full, rows), BF), shape((offsets, full, rows), BF)],
        1,
        (counts, feat, below, above, neighbors, weight_fine, slots),
        [pltpu.VMEM(((rows + 2 * halo) // LO * full, LO), BF), pltpu.VMEM((full, rows), F32)],
    )
    hidden_in = exchange(hidden_out)

    *fine_out, own_grad, to_below, to_above = call(
        functools.partial(backward_kernel, tiles, cw),
        [shape((fine_part, cw, full), BF)] * tiles
        + [shape((cw, rows), F32), shape((cw, halo), BF), shape((cw, halo), BF)],
        1,
        (place, slots, gate, picked, neighbors, wz, *slot_in),
        [
            pltpu.VMEM((blocks * full, LO), BF),
            pltpu.VMEM((full, rows), BF),
            pltpu.VMEM((tiles * fine_part, padded, full), F32),
            pltpu.VMEM(((rows + 2 * halo) // LO * padded, LO), F32),
        ],
    )
    from_above = lax.ppermute(to_below, "slab", down)
    from_below = lax.ppermute(to_above, "slab", up)
    fine_in = exchange(fine_out)

    coarse, *coarse_out = call(
        functools.partial(coarse_kernel, tiles, cap, capp),
        [shape((own, width), BF)] + [shape((coarse_part, own, full), BF)] * tiles,
        1,
        (place, children, weight_coarse, cotangent, *hidden_in),
        [
            pltpu.VMEM((blocks * full, LO), BF),
            pltpu.VMEM((kids, widep), jnp.int32),
            pltpu.VMEM((own, widep), BF),
            pltpu.VMEM((wide, widep), F32),
            pltpu.VMEM((tiles * coarse_part, own, full), F32),
        ],
    )
    coarse_in = exchange(coarse_out)

    grad_input = call(
        finish_kernel,
        shape((cw, rows), BF),
        1,
        (counts, own_grad, halo_rows.T, from_above, from_below),
    )
    scale = float(rows * tiles) ** (-0.5)
    fine_sum, coarse_sum = call(
        functools.partial(sum_kernel, tiles, scale),
        [shape((fine_part, cw, full), BF), shape((coarse_part, own, full), BF)],
        0,
        (*fine_in, *coarse_in),
    )
    grad_fine, grad_coarse = call(
        functools.partial(collect_kernel, tiles),
        [shape((offsets, cw, full), F32), shape((kids, own, full), F32)],
        1,
        (place, *spread(fine_sum, tiles), *spread(coarse_sum, tiles)),
    )
    return coarse, grad_fine, grad_coarse, grad_input


def solution(mesh):
    return jax.shard_map(
        local,
        mesh=mesh,
        in_specs=(
            P("chan", ("groups", "slab")),
            P(None, ("groups", "slab")),
            P(None, ("groups", "slab")),
            P(("groups", "slab")),
            P(("groups", "slab"), None),
            P(None, ("groups", "slab")),
            P(),
            P(),
            P("chan", ("groups", "slab")),
        ),
        out_specs=(
            P("chan", ("groups", "slab")),
            P("groups", "chan", None),
            P("groups", "chan", None),
            P("chan", ("groups", "slab")),
        ),
        check_vma=False,
    )
```

```python
import functools

import jax
import jax.numpy as jnp
from jax import lax
from jax.experimental import pallas as pl
from jax.experimental.pallas import tpu as pltpu
from jax.sharding import PartitionSpec as P

BF = jnp.bfloat16
F32 = jnp.float32
LO = 256
VMEM_LIMIT = 28 * 1024 * 1024
FLOPS_PER_US = 1_100_000_000


def up_to(value, step):
    return -(-value // step) * step


def dot(left, right):
    return jnp.dot(left, right, preferred_element_type=F32)


def dot_nt(left, right):
    return lax.dot_general(left, right, (((1,), (1,)), ((), ())), preferred_element_type=F32)


def dot_tn(left, right):
    return lax.dot_general(left, right, (((0,), (0,)), ((), ())), preferred_element_type=F32)


def one_hot(code, width=LO):
    low = code & (width - 1)
    rows = lax.broadcasted_iota(jnp.int32, (width, code.shape[1]), 0)
    return jnp.where(rows == low, 1.0, 0.0).astype(BF)


def gather_columns(blocks, code, channels):
    count = blocks.shape[0] // channels
    high = code >> 8
    found = dot(blocks, one_hot(code))
    picked = jnp.zeros((channels, code.shape[1]), F32)
    for block in range(count):
        picked = jnp.where(high == block, found[block * channels : (block + 1) * channels], picked)
    return picked.astype(BF)


def scatter_columns(values, code, count):
    high = code >> 8
    spread = jnp.concatenate(
        [values * jnp.where(high == block, 1.0, 0.0).astype(BF) for block in range(count)], axis=0
    )
    return dot_nt(spread, one_hot(code))


def split_slot(slots, cap, tiles):
    source = jnp.zeros_like(slots)
    for tile in range(1, tiles + 1):
        source = source + jnp.where(slots >= tile * cap, 1, 0)
    return source, slots - source * cap


def wrapped(value, tiles):
    return jnp.where(value < 0, value + tiles, value)


def own_rows(padded, full, cw, chan):
    line = lax.broadcasted_iota(jnp.int32, (padded, full), 0)
    column = lax.broadcasted_iota(jnp.int32, (padded, full), 1)
    return jnp.where((column == chan * cw + line) & (line < cw), 1.0, 0.0).astype(BF)


def unpack(refs, *counts):
    groups, start = [], 0
    for count in counts:
        groups.append(refs[start : start + count])
        start += count
    return (*groups, refs[start:])


def valid_row(count_ref, rows):
    return jnp.where(lax.broadcasted_iota(jnp.int32, (1, rows), 1) < count_ref[0], 1.0, 0.0)


def reordered(pieces, names, stack):
    part, width = pieces[0].shape
    size = part * len(pieces)
    column = lax.broadcasted_iota(jnp.int32, (1, size), 1)
    target = column
    for place, (piece, name) in enumerate(zip(pieces, names)):
        stack[place * part : (place + 1) * part, :width] = piece[...].astype(F32)
        inside = (column >= place * part) & (column < (place + 1) * part)
        target = jnp.where(inside, column + (name - place) * part, target)
    order = jnp.where(lax.broadcasted_iota(jnp.int32, (size, size), 0) == target, 1.0, 0.0)
    return dot(order.astype(BF), stack[...].astype(BF)).astype(BF)


def set_blocks(blocks_ref, table):
    channels = table.shape[0]
    for block in range(table.shape[1] // LO):
        blocks_ref[block * channels : (block + 1) * channels, :] = table[
            :, block * LO : (block + 1) * LO
        ]


def side_by_side(stacked, channels):
    return jnp.concatenate(
        [stacked[start : start + channels] for start in range(0, stacked.shape[0], channels)], axis=1
    )


def child_codes(code_pad, child, tile, sign, tiles, cap, capp):
    source, rank = split_slot(child, cap, tiles)
    code = wrapped(sign * (source - tile), tiles) * capp + rank
    code_pad[...] = jnp.full(code_pad.shape, tiles * capp, jnp.int32)
    code_pad[:, : child.shape[1]] = jnp.where(source == tiles, tiles * capp, code)


def gather_kernel(tiles, capp, pieces, *refs):
    (place_ref, count_ref, halo_ref, owner_ref), refs = refs[:4], refs[4:]
    feats, (feat_ref, low_ref, high_ref, slots_ref, feat_stack) = refs[:pieces], refs[pieces:]
    tile = place_ref[0]
    rows = feat_ref.shape[1]
    names = [place_ref[2 + piece] for piece in range(pieces)]
    valid = valid_row(count_ref, rows)
    table = (reordered(feats, names, feat_stack).astype(F32) * valid).astype(BF)
    feat_ref[...] = table
    width = halo_ref.shape[1]
    for side, out in ((0, low_ref), (1, high_ref)):
        picks = lax.broadcasted_iota(jnp.int32, (rows, width), 0) == halo_ref[side : side + 1, :]
        out[...] = dot(table, jnp.where(picks, 1.0, 0.0).astype(BF)).astype(BF)

    owner = owner_ref[...]
    bins, lanes = up_to(tiles, 16), 128
    same = jnp.where(lax.broadcasted_iota(jnp.int32, (bins, rows), 0) == owner, 1.0, 0.0)
    stacked = jnp.concatenate(
        [same[:, start : start + lanes] for start in range(0, rows, lanes)], axis=0
    )
    first = lax.broadcasted_iota(jnp.int32, (lanes, 2 * lanes), 0)
    second = lax.broadcasted_iota(jnp.int32, (lanes, 2 * lanes), 1)
    before = jnp.where((first < second) | (second >= lanes), 1.0, 0.0).astype(BF)
    earlier = dot(stacked.astype(BF), before)
    above = jnp.zeros((bins, lanes), F32)
    for block in range(rows // lanes):
        start = block * lanes
        lines = slice(block * bins, (block + 1) * bins)
        ranks = (earlier[lines, :lanes] + above) * same[:, start : start + lanes]
        rank = jnp.sum(ranks, axis=0, keepdims=True).astype(jnp.int32)
        above = above + earlier[lines, lanes:]
        name = owner[:, start : start + lanes]
        slots_ref[0:1, start : start + lanes] = wrapped(name - tile, tiles) * capp + rank
        slots_ref[1:2, start : start + lanes] = wrapped(tile - name, tiles) * capp + rank


def slot_kernel(tiles, cap, capp, cw, pieces, *refs):
    (place_ref, child_ref, wc_ref, wf_ref), refs = refs[:4], refs[4:]
    cots, outs, (wz_ref, cot_stack, code_pad, total) = unpack(refs, pieces, tiles)
    tile, chan = place_ref[0], place_ref[1]
    names = [place_ref[2 + piece] for piece in range(pieces)]
    kids = child_ref.shape[0]
    full = wf_ref.shape[2]
    blocks = tiles * capp // LO
    cot_stack[...] = jnp.zeros_like(cot_stack)
    cot = reordered(cots, names, cot_stack)
    child_codes(code_pad, child_ref[...], tile, 1, tiles, cap, capp)
    total[...] = jnp.zeros_like(total)
    step = 4 if kids % 4 == 0 else 1

    @pl.loop(0, kids // step)
    def _(group):
        terms = None
        for index in range(step):
            kid = group * step + index
            value = dot_tn(wc_ref[kid], cot).astype(BF)
            term = scatter_columns(value, code_pad[pl.ds(kid, 1), :], blocks)
            terms = term if terms is None else terms + term
        total[...] += terms

    sent = side_by_side(total[...].astype(BF), full)
    for step in range(tiles):
        outs[step][...] = sent[:, step * capp : (step + 1) * capp]
    own = own_rows(wz_ref.shape[1], full, cw, chan)
    for offset in range(wz_ref.shape[0]):
        wz_ref[offset] = dot_nt(own, wf_ref[offset]).astype(BF)


def steps_of(offsets):
    return 3 if offsets % 3 == 0 else 1


def forward_kernel(tiles, capp, *refs):
    (count_ref, feat_ref, below_ref, above_ref, slots_ref, nb_ref, wf_ref), refs = refs[:7], refs[7:]
    outs, refs = unpack(refs, tiles)
    gate_ref, picked_ref, blocks_ref = refs
    full, rows = feat_ref.shape
    offsets = nb_ref.shape[0]
    step = steps_of(offsets)
    set_blocks(blocks_ref, jnp.concatenate([feat_ref[...], below_ref[...], above_ref[...]], axis=1))

    @pl.loop(0, offsets // step)
    def _(group):
        for index in range(step):
            offset = group * step + index
            picked_ref[offset] = gather_columns(blocks_ref[...], nb_ref[pl.ds(offset, 1), :], full)

    pre = jnp.zeros((full, rows), F32)
    for offset in range(offsets):
        pre = pre + dot(wf_ref[offset], picked_ref[offset])
    valid = valid_row(count_ref, rows)
    gate_ref[...] = jnp.where(pre > 0, valid, 0.0).astype(BF)
    hidden = (jnp.maximum(pre, 0.0) * valid).astype(BF)
    placed = scatter_columns(hidden, slots_ref[0:1, :], tiles * capp // LO).astype(BF)
    outgoing = side_by_side(placed, full)
    for step in range(tiles):
        outs[step][...] = outgoing[:, step * capp : (step + 1) * capp]


def backward_kernel(tiles, cw, *refs):
    (place_ref, slots_ref, gate_ref, picked_ref, wz_ref, nb_ref), refs = refs[:6], refs[6:]
    takes, refs = unpack(refs, tiles)
    terms, own_ref, rim_ref, blocks_ref, grad_ref, total = refs
    chan = place_ref[1]
    full, rows = gate_ref.shape
    offsets = nb_ref.shape[0]
    padded = wz_ref.shape[1]
    step = steps_of(offsets)
    set_blocks(blocks_ref, jnp.concatenate([take[...] for take in takes], axis=1))
    grad = gather_columns(blocks_ref[...], slots_ref[1:2, :], full) * gate_ref[...]
    grad_ref[...] = grad
    own_grad = dot(own_rows(padded, full, cw, chan), grad).astype(BF)
    total[...] = jnp.zeros_like(total)
    for offset in range(offsets, terms.shape[0]):
        terms[offset] = jnp.zeros(terms.shape[1:], F32)
    count = total.shape[0] // padded

    @pl.loop(0, offsets // step)
    def _(group):
        first = group * step
        line = dot_nt(own_grad, picked_ref[pl.ds(first, step)].reshape(step * full, rows))
        values = dot(wz_ref[pl.ds(first, step)].reshape(step * padded, full), grad_ref[...])
        values = values.astype(BF)
        sums = None
        for index in range(step):
            terms[first + index] = line[:cw, index * full : (index + 1) * full]
            code = nb_ref[pl.ds(first + index, 1), :]
            part = scatter_columns(values[index * padded : (index + 1) * padded], code, count)
            sums = part if sums is None else sums + part
        total[...] += sums

    for block in range(rows // LO):
        own_ref[:, block * LO : (block + 1) * LO] = total[block * padded : block * padded + cw, :]
    lanes = rim_ref.shape[3]
    for side in range(2):
        for piece in range(rim_ref.shape[1]):
            start = rows + (side * rim_ref.shape[1] + piece) * lanes
            block, lane = start // LO, start % LO
            rim_ref[side, piece] = total[
                block * padded : block * padded + cw, lane : lane + lanes
            ].astype(BF)


def coarse_kernel(tiles, cap, capp, *refs):
    (place_ref, child_ref, cot_ref, fine_ref, rim_ref, wc_ref), refs = refs[:6], refs[6:]
    takes, (coarse_ref,), outs, refs = unpack(refs, tiles, 1, tiles)
    blocks_ref, code_pad, cot_pad, total, terms = refs
    tile, chan = place_ref[0], place_ref[1]
    kids, width = child_ref.shape
    full = wc_ref.shape[2]
    own = cot_ref.shape[0]
    cw = fine_ref.shape[1]
    ratio = own // cw
    fine_part = fine_ref.shape[0] // tiles
    coarse_part = terms.shape[0] // (tiles * ratio)
    cot_pad[...] = jnp.zeros_like(cot_pad)
    cot_pad[:, :width] = cot_ref[...]
    child_codes(code_pad, child_ref[...], tile, -1, tiles, cap, capp)
    set_blocks(blocks_ref, jnp.concatenate([take[...] for take in takes], axis=1))
    total[...] = jnp.zeros_like(total)
    for kid in range(kids * ratio, terms.shape[0]):
        terms[kid] = jnp.zeros(terms.shape[1:], F32)
    step = 4 if kids % 4 == 0 else 1

    @pl.loop(0, kids // step)
    def _(group):
        sums = None
        for index in range(step):
            kid = group * step + index
            picked = gather_columns(blocks_ref[...], code_pad[pl.ds(kid, 1), :], full)
            part = dot(wc_ref[kid], picked)
            sums = part if sums is None else sums + part
            line = dot_nt(cot_pad[...], picked)
            for piece in range(ratio):
                terms[kid * ratio + piece] = line[piece * cw : (piece + 1) * cw]
        total[...] += sums

    coarse_ref[...] = total[pl.ds(pl.multiple_of(chan * own, 8), own), :][:, :width].astype(BF)
    pieces = rim_ref.shape[1]
    for step in range(tiles):
        out = outs[step]
        out[...] = jnp.zeros_like(out)
        peer = lax.rem(tile + step, tiles)
        start = fine_part + coarse_part * ratio
        out[:fine_part, :, :full] = fine_ref[pl.ds(peer * fine_part, fine_part)].astype(BF)
        out[fine_part:start, :, :full] = terms[
            pl.ds(peer * coarse_part * ratio, coarse_part * ratio)
        ].astype(BF)
        if step == 1:
            out[start:] = rim_ref[1]
        if step == tiles - 1:
            out[start:] = rim_ref[0]


def finish_kernel(parts, place_ref, count_ref, own_ref, halo_ref, up_ref, down_ref, out_ref):
    rows = own_ref.shape[1]
    width = halo_ref.shape[1]
    tile, last = place_ref[0], place_ref[-1 + place_ref.shape[0]]
    total = own_ref[...]
    for side, take, there in ((1, down_ref, tile < last), (0, up_ref, tile > 0)):
        picks = lax.broadcasted_iota(jnp.int32, (rows, width), 0) == halo_ref[side : side + 1, :]
        hits = jnp.where(picks & there, 1.0, 0.0).astype(BF)
        rim = jnp.concatenate([take[parts + piece] for piece in range(take.shape[0] - parts)], axis=1)
        total = total + dot_nt(rim, hits)
    out_ref[...] = (total * valid_row(count_ref, rows)).astype(BF)


def sum_kernel(scale, *refs):
    takes, out = refs[:-1], refs[-1]
    total = takes[0][: out.shape[0]].astype(F32)
    for take in takes[1:]:
        total = total + take[: out.shape[0]].astype(F32)
    out[...] = (total * scale).astype(BF)


def collect_kernel(tiles, fine_part, place_ref, *refs):
    takes, (fine_ref, coarse_ref) = refs[:tiles], refs[tiles:]
    tile = place_ref[0]
    cw, full = fine_ref.shape[1:]
    ratio = coarse_ref.shape[1] // cw
    coarse_part = (takes[0].shape[0] - fine_part) // ratio
    for step in range(tiles):
        peer = lax.rem(tile + tiles - step, tiles)
        take = takes[step]
        for line in range(fine_part):
            index = peer * fine_part + line

            @pl.when(index < fine_ref.shape[0])
            def _(index=index, line=line, take=take):
                fine_ref[index] = take[line, :, :full].astype(F32)

        for line in range(coarse_part):
            index = peer * coarse_part + line

            @pl.when(index < coarse_ref.shape[0])
            def _(index=index, line=line, take=take):
                for piece in range(ratio):
                    coarse_ref[index, piece * cw : (piece + 1) * cw, :] = take[
                        fine_part + line * ratio + piece, :, :full
                    ].astype(F32)


def call(body, name, micros, outs, scalars, arrays, scratch=()):
    return pl.pallas_call(
        body,
        out_shape=outs,
        in_specs=[pl.BlockSpec(memory_space=pltpu.SMEM)] * len(scalars)
        + [pl.BlockSpec(memory_space=pltpu.VMEM)] * len(arrays),
        out_specs=jax.tree.map(lambda _: pl.BlockSpec(memory_space=pltpu.VMEM), outs),
        scratch_shapes=scratch,
        name=name,
        cost_estimate=pl.CostEstimate(
            flops=micros * FLOPS_PER_US, bytes_accessed=0, transcendentals=0
        ),
        compiler_params=pltpu.CompilerParams(vmem_limit_bytes=VMEM_LIMIT),
    )(*scalars, *arrays)


def exchange(chunks):
    tiles = len(chunks)
    if tiles <= 4:
        return [chunks[0]] + [
            lax.ppermute(chunks[step], "slab", [(i, (i + step) % tiles) for i in range(tiles)])
            for step in range(1, tiles)
        ]
    tile = lax.axis_index("slab")
    order = jnp.arange(tiles)
    stacked = jnp.take(jnp.stack(chunks), (order - tile) % tiles, axis=0)
    taken = lax.all_to_all(stacked, "slab", split_axis=0, concat_axis=0, tiled=True)
    taken = jnp.take(taken, (tile - order) % tiles, axis=0)
    return [taken[step] for step in range(tiles)]


def spread(chunk, tiles):
    return exchange([chunk] * tiles)


def pieces_of(block):
    count = lax.axis_size("chan")
    chan = lax.axis_index("chan")
    pair = [block]
    names = [chan]
    if count % 2 == 0:
        pair.append(lax.ppermute(block, "chan", [(i, i ^ 1) for i in range(count)]))
        names.append(chan ^ 1)
    found, sources = list(pair), list(names)
    width = len(pair)
    for step in range(width, count, width):
        moves = [(i, (i + step) % count) for i in range(count)]
        for piece, name in zip(pair, names):
            found.append(lax.ppermute(piece, "chan", moves))
            near = (chan - step) % count
            sources.append(near if name is chan else near ^ 1)
    return found, sources


def local(
    features, neighbors, halo_rows, counts, owners, children, weight_fine, weight_coarse, cotangent
):
    tiles = lax.axis_size("slab")
    tile, chan = lax.axis_index("slab"), lax.axis_index("chan")
    cw, rows = features.shape
    halo = halo_rows.shape[1]
    own, width = cotangent.shape
    offsets, full = weight_fine.shape[0], weight_fine.shape[2]
    kids, wide = weight_coarse.shape[0], weight_coarse.shape[1]
    cap = 9 * rows // (8 * tiles)
    capp = up_to(cap, 128)
    padded = up_to(cw, 16)
    widep = up_to(width, 128)
    blocks = tiles * capp // LO
    ratio = own // cw
    fine_part, coarse_part = -(-offsets // tiles), -(-kids // tiles)
    parts = fine_part + coarse_part * ratio
    rim = halo // 128
    shape = jax.ShapeDtypeStruct

    feats, names = pieces_of(features)
    cots, _ = pieces_of(cotangent)
    place = jnp.stack([tile, chan, *names, jnp.int32(tiles - 1)]).astype(jnp.int32)
    feat, low, high, slots = call(
        functools.partial(gather_kernel, tiles, capp, len(feats)),
        "gather",
        2,
        [shape((full, rows), BF)]
        + [shape((full, halo), BF)] * 2
        + [shape((8, rows), jnp.int32)],
        (place, counts),
        (halo_rows, owners.reshape(1, rows), *feats),
        [pltpu.VMEM((full, rows), F32)],
    )
    up = [(i, i + 1) for i in range(tiles - 1)]
    down = [(i + 1, i) for i in range(tiles - 1)]
    below = lax.ppermute(high, "slab", up)
    above = lax.ppermute(low, "slab", down)
    *slot_out, wz = call(
        functools.partial(slot_kernel, tiles, cap, capp, cw, len(cots)),
        "slots",
        5,
        [shape((full, capp), BF)] * tiles + [shape((offsets, padded, full), BF)],
        (place,),
        (children, weight_coarse, weight_fine, *cots),
        [
            pltpu.VMEM((wide, widep), F32),
            pltpu.VMEM((kids, widep), jnp.int32),
            pltpu.VMEM((blocks * full, LO), F32),
        ],
    )
    slot_in = exchange(slot_out)

    *hidden_out, gate, picked = call(
        functools.partial(forward_kernel, tiles, capp),
        "forward",
        12,
        [shape((full, capp), BF)] * tiles
        + [shape((full, rows), BF), shape((offsets, full, rows), BF)],
        (counts,),
        (feat, below, above, slots, neighbors, weight_fine),
        [pltpu.VMEM(((rows + 2 * halo) // LO * full, LO), BF)],
    )
    hidden_in = exchange(hidden_out)

    fine, own_grad, rims = call(
        functools.partial(backward_kernel, tiles, cw),
        "backward",
        9,
        [
            shape((tiles * fine_part, cw, full), F32),
            shape((cw, rows), F32),
            shape((2, rim, cw, 128), BF),
        ],
        (place,),
        (slots, gate, picked, wz, neighbors, *slot_in),
        [
            pltpu.VMEM((blocks * full, LO), BF),
            pltpu.VMEM((full, rows), BF),
            pltpu.VMEM(((rows + 2 * halo) // LO * padded, LO), F32),
        ],
    )

    coarse, *part_out = call(
        functools.partial(coarse_kernel, tiles, cap, capp),
        "coarse",
        6,
        [shape((own, width), BF)] + [shape((parts + rim, cw, 128), BF)] * tiles,
        (place,),
        (children, cotangent, fine, rims, weight_coarse, *hidden_in),
        [
            pltpu.VMEM((blocks * full, LO), BF),
            pltpu.VMEM((kids, widep), jnp.int32),
            pltpu.VMEM((own, widep), BF),
            pltpu.VMEM((wide, widep), F32),
            pltpu.VMEM((tiles * coarse_part * ratio, cw, full), F32),
        ],
    )
    part_in = exchange(part_out)

    scale = float(rows * tiles) ** (-0.5)
    part_sum = call(
        functools.partial(sum_kernel, scale), "sums", 1, shape((parts, cw, 128), BF), (), part_in
    )
    grad_input = call(
        functools.partial(finish_kernel, parts),
        "finish",
        2,
        shape((cw, rows), BF),
        (place, counts),
        (own_grad, halo_rows, part_in[1], part_in[tiles - 1]),
    )
    grad_fine, grad_coarse = call(
        functools.partial(collect_kernel, tiles, fine_part),
        "collect",
        1,
        [shape((offsets, cw, full), F32), shape((kids, own, full), F32)],
        (place,),
        spread(part_sum, tiles),
    )
    return coarse, grad_fine, grad_coarse, grad_input


def solution(mesh):
    return jax.shard_map(
        local,
        mesh=mesh,
        in_specs=(
            P("chan", ("groups", "slab")),
            P(None, ("groups", "slab")),
            P(None, ("groups", "slab")),
            P(("groups", "slab")),
            P(("groups", "slab"), None),
            P(None, ("groups", "slab")),
            P(),
            P(),
            P("chan", ("groups", "slab")),
        ),
        out_specs=(
            P("chan", ("groups", "slab")),
            P("groups", "chan", None),
            P("groups", "chan", None),
            P("chan", ("groups", "slab")),
        ),
        check_vma=False,
    )
```

```python
import functools

import jax
import jax.numpy as jnp
from jax import lax
from jax.experimental import pallas as pl
from jax.experimental.pallas import tpu as pltpu
from jax.sharding import PartitionSpec as P

BF = jnp.bfloat16
F32 = jnp.float32
LO = 256
VMEM_LIMIT = 28 * 1024 * 1024
FLOPS_PER_US = 1_100_000_000


def up_to(value, step):
    return -(-value // step) * step


def dot(left, right):
    return jnp.dot(left, right, preferred_element_type=F32)


def dot_nt(left, right):
    return lax.dot_general(left, right, (((1,), (1,)), ((), ())), preferred_element_type=F32)


def dot_tn(left, right):
    return lax.dot_general(left, right, (((0,), (0,)), ((), ())), preferred_element_type=F32)


def one_hot(code, width=LO):
    low = code & (width - 1)
    rows = lax.broadcasted_iota(jnp.int32, (width, code.shape[1]), 0)
    return jnp.where(rows == low, 1.0, 0.0).astype(BF)


def gather_columns(blocks, code, channels):
    count = blocks.shape[0] // channels
    high = code >> 8
    found = dot(blocks, one_hot(code))
    picked = jnp.zeros((channels, code.shape[1]), F32)
    for block in range(count):
        picked = jnp.where(high == block, found[block * channels : (block + 1) * channels], picked)
    return picked.astype(BF)


def scatter_columns(values, code, count):
    high = code >> 8
    spread = jnp.concatenate(
        [values * jnp.where(high == block, 1.0, 0.0).astype(BF) for block in range(count)], axis=0
    )
    return dot_nt(spread, one_hot(code))


def split_slot(slots, cap, tiles):
    source = jnp.zeros_like(slots)
    for tile in range(1, tiles + 1):
        source = source + jnp.where(slots >= tile * cap, 1, 0)
    return source, slots - source * cap


def wrapped(value, tiles):
    return jnp.where(value < 0, value + tiles, value)


def pair_rows(lines, full, cw, chan):
    line = lax.broadcasted_iota(jnp.int32, (lines, full), 0)
    column = lax.broadcasted_iota(jnp.int32, (lines, full), 1)
    target = jnp.where(line < cw, chan * cw + line, (chan ^ 1) * cw + line - cw)
    return jnp.where((column == target) & (line < 2 * cw), 1.0, 0.0).astype(BF)


def half_of(chan, rows):
    half = rows // 2
    return pl.multiple_of((chan & 1) * half, half), pl.multiple_of((1 - (chan & 1)) * half, half)


def unpack(refs, *counts):
    groups, start = [], 0
    for count in counts:
        groups.append(refs[start : start + count])
        start += count
    return (*groups, refs[start:])


def valid_row(count_ref, rows):
    return jnp.where(lax.broadcasted_iota(jnp.int32, (1, rows), 1) < count_ref[0], 1.0, 0.0)


def reordered(pieces, names, stack):
    part, width = pieces[0].shape
    size = part * len(pieces)
    column = lax.broadcasted_iota(jnp.int32, (1, size), 1)
    target = column
    for place, (piece, name) in enumerate(zip(pieces, names)):
        stack[place * part : (place + 1) * part, :width] = piece[...].astype(F32)
        inside = (column >= place * part) & (column < (place + 1) * part)
        target = jnp.where(inside, column + (name - place) * part, target)
    order = jnp.where(lax.broadcasted_iota(jnp.int32, (size, size), 0) == target, 1.0, 0.0)
    return dot(order.astype(BF), stack[...].astype(BF)).astype(BF)


def set_blocks(blocks_ref, table):
    channels = table.shape[0]
    for block in range(table.shape[1] // LO):
        blocks_ref[block * channels : (block + 1) * channels, :] = table[
            :, block * LO : (block + 1) * LO
        ]


def side_by_side(stacked, channels):
    return jnp.concatenate(
        [stacked[start : start + channels] for start in range(0, stacked.shape[0], channels)], axis=1
    )


def child_codes(code_pad, child, tile, sign, tiles, cap, capp):
    source, rank = split_slot(child, cap, tiles)
    code = wrapped(sign * (source - tile), tiles) * capp + rank
    code_pad[...] = jnp.full(code_pad.shape, tiles * capp, jnp.int32)
    code_pad[:, : child.shape[1]] = jnp.where(source == tiles, tiles * capp, code)


def gather_kernel(tiles, capp, pieces, *refs):
    (place_ref, count_ref, meta_ref), refs = refs[:3], refs[3:]
    feats, (feat_ref, low_ref, high_ref, slots_ref, feat_stack) = refs[:pieces], refs[pieces:]
    tile = place_ref[0]
    rows = feat_ref.shape[1]
    names = [place_ref[2 + piece] for piece in range(pieces)]
    valid = valid_row(count_ref, rows)
    table = (reordered(feats, names, feat_stack).astype(F32) * valid).astype(BF)
    feat_ref[...] = table
    width = low_ref.shape[1]
    for side, out in ((0, low_ref), (1, high_ref)):
        chosen = meta_ref[0:1, side * width : (side + 1) * width]
        picks = lax.broadcasted_iota(jnp.int32, (rows, width), 0) == chosen
        out[...] = dot(table, jnp.where(picks, 1.0, 0.0).astype(BF)).astype(BF)

    owner = meta_ref[0:1, 2 * width :]
    bins, lanes = up_to(tiles, 16), 128
    same = jnp.where(lax.broadcasted_iota(jnp.int32, (bins, rows), 0) == owner, 1.0, 0.0)
    stacked = jnp.concatenate(
        [same[:, start : start + lanes] for start in range(0, rows, lanes)], axis=0
    )
    first = lax.broadcasted_iota(jnp.int32, (lanes, 2 * lanes), 0)
    second = lax.broadcasted_iota(jnp.int32, (lanes, 2 * lanes), 1)
    before = jnp.where((first < second) | (second >= lanes), 1.0, 0.0).astype(BF)
    earlier = dot(stacked.astype(BF), before)
    above = jnp.zeros((bins, lanes), F32)
    for block in range(rows // lanes):
        start = block * lanes
        lines = slice(block * bins, (block + 1) * bins)
        ranks = (earlier[lines, :lanes] + above) * same[:, start : start + lanes]
        rank = jnp.sum(ranks, axis=0, keepdims=True).astype(jnp.int32)
        above = above + earlier[lines, lanes:]
        name = owner[:, start : start + lanes]
        slots_ref[0:1, start : start + lanes] = wrapped(name - tile, tiles) * capp + rank
        slots_ref[1:2, start : start + lanes] = wrapped(tile - name, tiles) * capp + rank


def select_kernel(cw, place_ref, wf_ref, wz_ref):
    own = pair_rows(wz_ref.shape[1], wz_ref.shape[2], cw, place_ref[1])
    for offset in range(wz_ref.shape[0]):
        wz_ref[offset] = dot_nt(own, wf_ref[offset]).astype(BF)


def slot_kernel(tiles, cap, capp, pieces, *refs):
    (place_ref, child_ref, wc_ref), refs = refs[:3], refs[3:]
    cots, outs, (cot_stack, code_pad, total) = unpack(refs, pieces, tiles)
    tile = place_ref[0]
    names = [place_ref[2 + piece] for piece in range(pieces)]
    kids = child_ref.shape[0]
    full = wc_ref.shape[2]
    blocks = tiles * capp // LO
    cot_stack[...] = jnp.zeros_like(cot_stack)
    cot = reordered(cots, names, cot_stack)
    child_codes(code_pad, child_ref[...], tile, 1, tiles, cap, capp)
    total[...] = jnp.zeros_like(total)
    for first in range(0, kids, 2):
        pair = (first, first + 1)
        value = jnp.concatenate([dot_tn(wc_ref[kid], cot).astype(BF) for kid in pair], axis=1)
        code = jnp.concatenate([code_pad[kid : kid + 1, :] for kid in pair], axis=1)
        total[...] += scatter_columns(value, code, blocks)

    sent = side_by_side(total[...].astype(BF), full)
    for step in range(tiles):
        outs[step][...] = sent[:, step * capp : (step + 1) * capp]


def forward_kernel(place_ref, count_ref, feat_ref, below_ref, above_ref, nb_ref, wf_ref, *refs):
    hidden_ref, gate_ref, picked_ref, blocks_ref = refs
    full, rows = feat_ref.shape
    half = rows // 2
    start, _ = half_of(place_ref[1], rows)
    offsets = nb_ref.shape[0]
    step = 9 if offsets % 9 == 0 else 1
    set_blocks(blocks_ref, jnp.concatenate([feat_ref[...], below_ref[...], above_ref[...]], axis=1))

    @pl.loop(0, offsets // step)
    def _(group):
        for index in range(step):
            offset = group * step + index
            code = nb_ref[pl.ds(offset, 1), pl.ds(start, half)]
            picked_ref[offset] = gather_columns(blocks_ref[...], code, full)

    pre = jnp.zeros((full, half), F32)
    for offset in range(offsets):
        pre = pre + dot(wf_ref[offset], picked_ref[offset])
    line = start + lax.broadcasted_iota(jnp.int32, (1, half), 1)
    valid = jnp.where(line < count_ref[0], 1.0, 0.0)
    gate_ref[...] = jnp.where(pre > 0, valid, 0.0).astype(BF)
    hidden_ref[...] = (jnp.maximum(pre, 0.0) * valid).astype(BF)


def place_kernel(tiles, capp, place_ref, slots_ref, own_ref, other_ref, *outs):
    full, half = own_ref.shape
    start, other = half_of(place_ref[1], 2 * half)
    hidden = jnp.concatenate([own_ref[...], other_ref[...]], axis=1)
    code = jnp.concatenate(
        [slots_ref[0:1, pl.ds(start, half)], slots_ref[0:1, pl.ds(other, half)]], axis=1
    )
    placed = scatter_columns(hidden, code, tiles * capp // LO).astype(BF)
    outgoing = side_by_side(placed, full)
    for step in range(tiles):
        outs[step][...] = outgoing[:, step * capp : (step + 1) * capp]


def backward_kernel(tiles, cw, *refs):
    (place_ref, slots_ref, gate_ref, picked_ref, wz_ref, nb_ref), refs = refs[:6], refs[6:]
    takes, refs = unpack(refs, tiles)
    terms, other_terms, table_ref, other_table, blocks_ref, grad_ref, total = refs
    chan = place_ref[1]
    full, half = gate_ref.shape
    start, _ = half_of(chan, 2 * half)
    offsets = nb_ref.shape[0]
    padded = wz_ref.shape[1]
    step = 3 if offsets % 3 == 0 else 1
    set_blocks(blocks_ref, jnp.concatenate([take[...] for take in takes], axis=1))
    code = slots_ref[1:2, pl.ds(start, half)]
    grad = gather_columns(blocks_ref[...], code, full) * gate_ref[...]
    grad_ref[...] = grad
    pair_grad = dot(pair_rows(padded, full, cw, chan), grad).astype(BF)
    total[...] = jnp.zeros_like(total)
    for offset in range(offsets, terms.shape[0]):
        terms[offset] = jnp.zeros(terms.shape[1:], F32)
        other_terms[offset] = jnp.zeros(terms.shape[1:], BF)
    count = total.shape[0] // padded

    @pl.loop(0, offsets // step)
    def _(group):
        first = group * step
        line = dot_nt(pair_grad, picked_ref[pl.ds(first, step)].reshape(step * full, half))
        values = dot(wz_ref[pl.ds(first, step)].reshape(step * padded, full), grad_ref[...])
        values = values.astype(BF)
        sums = None
        for index in range(step):
            part = line[:, index * full : (index + 1) * full]
            terms[first + index] = part[:cw]
            other_terms[first + index] = part[cw : 2 * cw].astype(BF)
            code = nb_ref[pl.ds(first + index, 1), pl.ds(start, half)]
            part = scatter_columns(values[index * padded : (index + 1) * padded], code, count)
            sums = part if sums is None else sums + part
        total[...] += sums

    for block in range(count):
        lanes = slice(block * LO, (block + 1) * LO)
        first = block * padded
        table_ref[:, lanes] = total[first : first + cw, :]
        other_table[:, lanes] = total[first + cw : first + 2 * cw, :].astype(BF)


def child_kernel(tiles, cap, capp, ratio, *refs):
    (place_ref, child_ref, cot_ref), refs = refs[:3], refs[3:]
    takes, (picked_ref, terms), refs = unpack(refs, tiles, 2)
    blocks_ref, code_pad, cot_pad = refs
    kids, width = child_ref.shape
    full = picked_ref.shape[1]
    cw = cot_ref.shape[0] // ratio
    cot_pad[...] = jnp.zeros_like(cot_pad)
    cot_pad[:, :width] = cot_ref[...]
    child_codes(code_pad, child_ref[...], place_ref[0], -1, tiles, cap, capp)
    set_blocks(blocks_ref, jnp.concatenate([take[...] for take in takes], axis=1))
    for line in range(kids * ratio, terms.shape[0]):
        terms[line] = jnp.zeros(terms.shape[1:], F32)
    wide = code_pad.shape[1]
    for first in range(0, kids, 2):
        code = jnp.concatenate([code_pad[kid : kid + 1, :] for kid in (first, first + 1)], axis=1)
        both = gather_columns(blocks_ref[...], code, full)
        for kid in (first, first + 1):
            picked = both[:, (kid - first) * wide : (kid - first + 1) * wide]
            picked_ref[kid] = picked
            line = dot_nt(cot_pad[...], picked)
            for piece in range(ratio):
                terms[kid * ratio + piece] = line[piece * cw : (piece + 1) * cw]


def coarse_kernel(place_ref, picked_ref, wc_ref, coarse_ref, total):
    own, width = coarse_ref.shape
    sums = None
    for kid in range(picked_ref.shape[0]):
        part = dot(wc_ref[kid], picked_ref[kid])
        sums = part if sums is None else sums + part
    total[...] = sums
    start = pl.multiple_of(place_ref[1] * own, 8)
    coarse_ref[...] = total[pl.ds(start, own), :][:, :width].astype(BF)


def pack_kernel(tiles, *refs):
    (place_ref, fine_ref, fine_other, table_ref, table_other, terms), refs = refs[:6], refs[6:]
    outs, (own_ref,) = refs[:tiles], refs[tiles:]
    tile = place_ref[0]
    full = fine_ref.shape[2]
    rows = own_ref.shape[1]
    rim = (table_ref.shape[1] - rows) // 2
    fine_part = fine_ref.shape[0] // tiles
    coarse_part = terms.shape[0] // tiles
    used = (fine_part + coarse_part) * full
    base = up_to(used, 128)
    own_ref[...] = table_ref[:, :rows] + table_other[:, :rows].astype(F32)
    for step in range(tiles):
        out = outs[step]
        out[...] = jnp.zeros_like(out)
        peer = lax.rem(tile + step, tiles)
        fine = pl.ds(peer * fine_part, fine_part)
        fines = fine_ref[fine] + fine_other[fine].astype(F32)
        coarses = terms[pl.ds(peer * coarse_part, coarse_part)]
        units = [fines[unit] for unit in range(fine_part)]
        units += [coarses[unit] for unit in range(coarse_part)]
        out[:, :used] = jnp.concatenate(units, axis=1).astype(BF)
        for side in range(2):
            if step == (tiles - 1, 1)[side]:
                lanes = slice(rows + side * rim, rows + (side + 1) * rim)
                out[:, base : base + rim] = (
                    table_ref[:, lanes] + table_other[:, lanes].astype(F32)
                ).astype(BF)


def finish_kernel(place_ref, count_ref, own_ref, halo_ref, up_ref, down_ref, out_ref):
    rows = own_ref.shape[1]
    width = halo_ref.shape[1]
    base = up_ref.shape[1] - width
    tile, last = place_ref[0], place_ref[-1 + place_ref.shape[0]]
    total = own_ref[...]
    for side, take, there in ((1, down_ref, tile < last), (0, up_ref, tile > 0)):
        picks = lax.broadcasted_iota(jnp.int32, (rows, width), 0) == halo_ref[side : side + 1, :]
        hits = jnp.where(picks & there, 1.0, 0.0).astype(BF)
        total = total + dot_nt(take[:, base:], hits)
    out_ref[...] = (total * valid_row(count_ref, rows)).astype(BF)


def sum_kernel(scale, *refs):
    takes, out = refs[:-1], refs[-1]
    width = out.shape[1]
    total = takes[0][:, :width].astype(F32)
    for take in takes[1:]:
        total = total + take[:, :width].astype(F32)
    out[...] = (total * scale).astype(BF)


def collect_kernel(tiles, fine_part, place_ref, *refs):
    takes, (fine_ref, coarse_ref) = refs[:tiles], refs[tiles:]
    tile = place_ref[0]
    cw, full = fine_ref.shape[1:]
    ratio = coarse_ref.shape[1] // cw
    coarse_part = -(-coarse_ref.shape[0] // tiles)
    for step in range(tiles):
        peer = lax.rem(tile + tiles - step, tiles)
        take = takes[step][...].astype(F32)
        units = [
            take[:, unit * full : (unit + 1) * full]
            for unit in range(fine_part + coarse_part * ratio)
        ]
        for line in range(fine_part):
            index = peer * fine_part + line

            @pl.when(index < fine_ref.shape[0])
            def _(index=index, unit=units[line]):
                fine_ref[index] = unit

        for line in range(coarse_part):
            index = peer * coarse_part + line

            @pl.when(index < coarse_ref.shape[0])
            def _(index=index, first=fine_part + line * ratio, units=units):
                for piece in range(ratio):
                    coarse_ref[index, piece * cw : (piece + 1) * cw, :] = units[first + piece]


def call(body, name, micros, outs, scalars, arrays, scratch=()):
    return pl.pallas_call(
        body,
        out_shape=outs,
        in_specs=[pl.BlockSpec(memory_space=pltpu.SMEM)] * len(scalars)
        + [pl.BlockSpec(memory_space=pltpu.VMEM)] * len(arrays),
        out_specs=jax.tree.map(lambda _: pl.BlockSpec(memory_space=pltpu.VMEM), outs),
        scratch_shapes=scratch,
        name=name,
        cost_estimate=pl.CostEstimate(
            flops=micros * FLOPS_PER_US, bytes_accessed=0, transcendentals=0
        ),
        compiler_params=pltpu.CompilerParams(vmem_limit_bytes=VMEM_LIMIT),
    )(*scalars, *arrays)


def exchange(chunks):
    tiles = len(chunks)
    if tiles <= 4:
        return [chunks[0]] + [
            lax.ppermute(chunks[step], "slab", [(i, (i + step) % tiles) for i in range(tiles)])
            for step in range(1, tiles)
        ]
    tile = lax.axis_index("slab")
    order = jnp.arange(tiles)
    stacked = jnp.take(jnp.stack(chunks), (order - tile) % tiles, axis=0)
    taken = lax.all_to_all(stacked, "slab", split_axis=0, concat_axis=0, tiled=True)
    taken = jnp.take(taken, (tile - order) % tiles, axis=0)
    return [taken[step] for step in range(tiles)]


def other_core(block):
    count = lax.axis_size("chan")
    return lax.ppermute(block, "chan", [(i, i ^ 1) for i in range(count)])


def spread(chunk, tiles):
    return exchange([chunk] * tiles)


def pieces_of(block):
    count = lax.axis_size("chan")
    chan = lax.axis_index("chan")
    found, sources = [block], [chan]
    for step in range(2, count, 2):
        moves = [(i, (i + step) % count) for i in range(count)]
        found.append(lax.ppermute(block, "chan", moves))
        sources.append((chan - step) % count)
    return found + [other_core(piece) for piece in found], sources + [name ^ 1 for name in sources]


def local(
    features, neighbors, halo_rows, counts, owners, children, weight_fine, weight_coarse, cotangent
):
    tiles = lax.axis_size("slab")
    tile, chan = lax.axis_index("slab"), lax.axis_index("chan")
    cw, rows = features.shape
    halo = halo_rows.shape[1]
    own, width = cotangent.shape
    offsets, full = weight_fine.shape[0], weight_fine.shape[2]
    kids, wide = weight_coarse.shape[0], weight_coarse.shape[1]
    cap = 9 * rows // (8 * tiles)
    capp = up_to(cap, 128)
    padded = up_to(2 * cw, 16)
    half = rows // 2
    ext = rows + 2 * halo
    widep = up_to(width, 128)
    blocks = tiles * capp // LO
    ratio = own // cw
    fine_part, coarse_part = -(-offsets // tiles), -(-kids // tiles)
    parts = fine_part + coarse_part * ratio
    base = up_to(parts * full, 128)
    shape = jax.ShapeDtypeStruct

    feats, names = pieces_of(features)
    place = jnp.stack([tile, chan, *names, jnp.int32(tiles - 1)]).astype(jnp.int32)
    masked = jnp.where(jnp.arange(rows) < counts[0], features, 0).astype(BF)
    meta = jnp.concatenate([halo_rows.reshape(1, 2 * halo), owners.reshape(1, rows)], axis=1)
    wz = call(
        functools.partial(select_kernel, cw),
        "select",
        3,
        shape((offsets, padded, full), BF),
        (place,),
        (weight_fine,),
    )
    feat, low, high, slots = call(
        functools.partial(gather_kernel, tiles, capp, len(feats)),
        "gather",
        2,
        [shape((full, rows), BF)]
        + [shape((full, halo), BF)] * 2
        + [shape((8, rows), jnp.int32)],
        (place, counts),
        (meta, masked, *feats[1:]),
        [pltpu.VMEM((full, rows), F32)],
    )
    up = [(i, i + 1) for i in range(tiles - 1)]
    down = [(i + 1, i) for i in range(tiles - 1)]
    late, low, high = lax.optimization_barrier((cotangent, low, high))
    cots, _ = pieces_of(late)
    below = lax.ppermute(high, "slab", up)
    above = lax.ppermute(low, "slab", down)
    slot_out = call(
        functools.partial(slot_kernel, tiles, cap, capp, len(feats)),
        "slots",
        5,
        [shape((full, capp), BF)] * tiles,
        (place,),
        (children, weight_coarse, *cots),
        [
            pltpu.VMEM((wide, widep), F32),
            pltpu.VMEM((kids, widep), jnp.int32),
            pltpu.VMEM((blocks * full, LO), F32),
        ],
    )
    slot_in = exchange(slot_out)

    hidden, gate, picked = call(
        forward_kernel,
        "forward",
        7,
        [shape((full, half), BF)] * 2 + [shape((offsets, full, half), BF)],
        (place, counts),
        (feat, below, above, neighbors, weight_fine),
        [pltpu.VMEM((ext // LO * full, LO), BF)],
    )
    hidden_out = call(
        functools.partial(place_kernel, tiles, capp),
        "place",
        1,
        [shape((full, capp), BF)] * tiles,
        (place,),
        (slots, hidden, other_core(hidden)),
    )
    hidden_in = exchange(hidden_out)

    fine, other_fine, table, other_table = call(
        functools.partial(backward_kernel, tiles, cw),
        "backward",
        6,
        [
            shape((tiles * fine_part, cw, full), F32),
            shape((tiles * fine_part, cw, full), BF),
            shape((cw, ext), F32),
            shape((cw, ext), BF),
        ],
        (place,),
        (slots, gate, picked, wz, neighbors, *slot_in),
        [
            pltpu.VMEM((blocks * full, LO), BF),
            pltpu.VMEM((full, half), BF),
            pltpu.VMEM((ext // LO * padded, LO), F32),
        ],
    )
    other_fine, other_table = other_core(other_fine), other_core(other_table)

    kept, terms = call(
        functools.partial(child_kernel, tiles, cap, capp, ratio),
        "children",
        4,
        [shape((kids, full, widep), BF), shape((tiles * coarse_part * ratio, cw, full), F32)],
        (place,),
        (children, cotangent, *hidden_in),
        [
            pltpu.VMEM((blocks * full, LO), BF),
            pltpu.VMEM((kids, widep), jnp.int32),
            pltpu.VMEM((own, widep), BF),
        ],
    )
    *part_out, own_grad = call(
        functools.partial(pack_kernel, tiles),
        "pack",
        1,
        [
            shape((cw, base + (halo if tiles > 4 or step in (1, tiles - 1) else 0)), BF)
            for step in range(tiles)
        ]
        + [shape((cw, rows), F32)],
        (place,),
        (fine, other_fine, table, other_table, terms),
    )
    part_in = exchange(part_out)
    coarse = call(
        coarse_kernel,
        "coarse",
        2,
        shape((own, width), BF),
        (place,),
        (kept, weight_coarse),
        [pltpu.VMEM((wide, widep), F32)],
    )

    scale = float(rows * tiles) ** (-0.5)
    part_sum = call(
        functools.partial(sum_kernel, scale), "sums", 1, shape((cw, base), BF), (), part_in
    )
    grad_input = call(
        finish_kernel,
        "finish",
        2,
        shape((cw, rows), BF),
        (place, counts),
        (own_grad, halo_rows, part_in[1], part_in[tiles - 1]),
    )
    grad_fine, grad_coarse = call(
        functools.partial(collect_kernel, tiles, fine_part),
        "collect",
        1,
        [shape((offsets, cw, full), F32), shape((kids, own, full), F32)],
        (place,),
        spread(part_sum, tiles),
    )
    return coarse, grad_fine, grad_coarse, grad_input


def solution(mesh):
    return jax.shard_map(
        local,
        mesh=mesh,
        in_specs=(
            P("chan", ("groups", "slab")),
            P(None, ("groups", "slab")),
            P(None, ("groups", "slab")),
            P(("groups", "slab")),
            P(("groups", "slab"), None),
            P(None, ("groups", "slab")),
            P(),
            P(),
            P("chan", ("groups", "slab")),
        ),
        out_specs=(
            P("chan", ("groups", "slab")),
            P("groups", "chan", None),
            P("groups", "chan", None),
            P("chan", ("groups", "slab")),
        ),
        check_vma=False,
    )
```

```python
import functools

import jax
import jax.numpy as jnp
from jax import lax
from jax.experimental import pallas as pl
from jax.experimental.pallas import tpu as pltpu
from jax.sharding import PartitionSpec as P

BF = jnp.bfloat16
F32 = jnp.float32
LO = 256
VMEM_LIMIT = 28 * 1024 * 1024
FLOPS_PER_US = 1_100_000_000


def up_to(value, step):
    return -(-value // step) * step


def dot(left, right):
    return jnp.dot(left, right, preferred_element_type=F32)


def dot_nt(left, right):
    return lax.dot_general(left, right, (((1,), (1,)), ((), ())), preferred_element_type=F32)


def dot_tn(left, right):
    return lax.dot_general(left, right, (((0,), (0,)), ((), ())), preferred_element_type=F32)


def one_hot(code, width=LO):
    low = code & (width - 1)
    rows = lax.broadcasted_iota(jnp.int32, (width, code.shape[1]), 0)
    return jnp.where(rows == low, 1.0, 0.0).astype(BF)


def gather_columns(blocks, code, channels):
    count = blocks.shape[0] // channels
    high = code >> 8
    found = dot(blocks, one_hot(code))
    picked = jnp.zeros((channels, code.shape[1]), F32)
    for block in range(count):
        picked = jnp.where(high == block, found[block * channels : (block + 1) * channels], picked)
    return picked.astype(BF)


def scatter_columns(values, code, count):
    high = code >> 8
    spread = jnp.concatenate(
        [values * jnp.where(high == block, 1.0, 0.0).astype(BF) for block in range(count)], axis=0
    )
    return dot_nt(spread, one_hot(code))


def split_slot(slots, cap, tiles):
    source = jnp.zeros_like(slots)
    for tile in range(1, tiles + 1):
        source = source + jnp.where(slots >= tile * cap, 1, 0)
    return source, slots - source * cap


def edge_pairs(tiles):
    first = [(i, i + 1) for i in range(0, tiles - 1, 2)]
    second = [(i, i + 1) for i in range(1, tiles - 1, 2)]
    return [pairs + [(j, i) for i, j in pairs] for pairs in (first, second)]


def wrapped(value, tiles):
    return jnp.where(value < 0, value + tiles, value)


def pair_rows(lines, full, cw, chan):
    line = lax.broadcasted_iota(jnp.int32, (lines, full), 0)
    column = lax.broadcasted_iota(jnp.int32, (lines, full), 1)
    target = jnp.where(line < cw, chan * cw + line, (chan ^ 1) * cw + line - cw)
    return jnp.where((column == target) & (line < 2 * cw), 1.0, 0.0).astype(BF)


def half_of(chan, rows):
    half = rows // 2
    return pl.multiple_of((chan & 1) * half, half), pl.multiple_of((1 - (chan & 1)) * half, half)


def unpack(refs, *counts):
    groups, start = [], 0
    for count in counts:
        groups.append(refs[start : start + count])
        start += count
    return (*groups, refs[start:])


def valid_row(count_ref, rows):
    return jnp.where(lax.broadcasted_iota(jnp.int32, (1, rows), 1) < count_ref[0], 1.0, 0.0)


def reordered(pieces, names, stack):
    part, width = pieces[0].shape
    size = part * len(pieces)
    column = lax.broadcasted_iota(jnp.int32, (1, size), 1)
    target = column
    for place, (piece, name) in enumerate(zip(pieces, names)):
        stack[place * part : (place + 1) * part, :width] = piece[...].astype(F32)
        inside = (column >= place * part) & (column < (place + 1) * part)
        target = jnp.where(inside, column + (name - place) * part, target)
    order = jnp.where(lax.broadcasted_iota(jnp.int32, (size, size), 0) == target, 1.0, 0.0)
    return dot(order.astype(BF), stack[...].astype(BF)).astype(BF)


def set_blocks(blocks_ref, table):
    channels = table.shape[0]
    for block in range(table.shape[1] // LO):
        blocks_ref[block * channels : (block + 1) * channels, :] = table[
            :, block * LO : (block + 1) * LO
        ]


def side_by_side(stacked, channels):
    return jnp.concatenate(
        [stacked[start : start + channels] for start in range(0, stacked.shape[0], channels)], axis=1
    )


def child_codes(code_pad, child, tile, sign, tiles, cap, capp):
    source, rank = split_slot(child, cap, tiles)
    code = wrapped(sign * (source - tile), tiles) * capp + rank
    code_pad[...] = jnp.full(code_pad.shape, tiles * capp, jnp.int32)
    code_pad[:, : child.shape[1]] = jnp.where(source == tiles, tiles * capp, code)


def gather_kernel(pieces, *refs):
    (place_ref, count_ref, halo_ref), refs = refs[:3], refs[3:]
    feats, (feat_ref, first_ref, second_ref, feat_stack) = refs[:pieces], refs[pieces:]
    tile = place_ref[0]
    rows = feat_ref.shape[1]
    names = [place_ref[2 + piece] for piece in range(pieces)]
    valid = valid_row(count_ref, rows)
    table = (reordered(feats, names, feat_stack).astype(F32) * valid).astype(BF)
    feat_ref[...] = table
    width = first_ref.shape[1]
    odd = tile & 1
    lower, upper = halo_ref[0:1, :], halo_ref[1:2, :]
    for side, out in ((0, first_ref), (1, second_ref)):
        chosen = jnp.where(odd == side, upper, lower)
        picks = lax.broadcasted_iota(jnp.int32, (rows, width), 0) == chosen
        out[...] = dot(table, jnp.where(picks, 1.0, 0.0).astype(BF)).astype(BF)


def select_kernel(tiles, capp, cw, place_ref, owner_ref, wf_ref, slots_ref, wz_ref):
    tile = place_ref[0]
    owner = owner_ref[...]
    rows = owner.shape[1]
    bins, lanes = up_to(tiles, 16), 128
    same = jnp.where(lax.broadcasted_iota(jnp.int32, (bins, rows), 0) == owner, 1.0, 0.0)
    stacked = jnp.concatenate(
        [same[:, start : start + lanes] for start in range(0, rows, lanes)], axis=0
    )
    first = lax.broadcasted_iota(jnp.int32, (lanes, 2 * lanes), 0)
    second = lax.broadcasted_iota(jnp.int32, (lanes, 2 * lanes), 1)
    before = jnp.where((first < second) | (second >= lanes), 1.0, 0.0).astype(BF)
    earlier = dot(stacked.astype(BF), before)
    above = jnp.zeros((bins, lanes), F32)
    for block in range(rows // lanes):
        start = block * lanes
        lines = slice(block * bins, (block + 1) * bins)
        ranks = (earlier[lines, :lanes] + above) * same[:, start : start + lanes]
        rank = jnp.sum(ranks, axis=0, keepdims=True).astype(jnp.int32)
        above = above + earlier[lines, lanes:]
        name = owner[:, start : start + lanes]
        slots_ref[0:1, start : start + lanes] = wrapped(name - tile, tiles) * capp + rank
        slots_ref[1:2, start : start + lanes] = wrapped(tile - name, tiles) * capp + rank
    own = pair_rows(wz_ref.shape[1], wz_ref.shape[2], cw, place_ref[1])
    for offset in range(wz_ref.shape[0]):
        wz_ref[offset] = dot_nt(own, wf_ref[offset]).astype(BF)


def slot_kernel(tiles, cap, capp, pieces, *refs):
    (place_ref, child_ref, wc_ref), refs = refs[:3], refs[3:]
    cots, outs, (cot_stack, code_pad, total) = unpack(refs, pieces, tiles)
    tile = place_ref[0]
    names = [place_ref[2 + piece] for piece in range(pieces)]
    kids = child_ref.shape[0]
    full = wc_ref.shape[2]
    blocks = tiles * capp // LO
    cot_stack[...] = jnp.zeros_like(cot_stack)
    cot = reordered(cots, names, cot_stack)
    child_codes(code_pad, child_ref[...], tile, 1, tiles, cap, capp)
    total[...] = jnp.zeros_like(total)
    for first in range(0, kids, 2):
        pair = (first, first + 1)
        value = jnp.concatenate([dot_tn(wc_ref[kid], cot).astype(BF) for kid in pair], axis=1)
        code = jnp.concatenate([code_pad[kid : kid + 1, :] for kid in pair], axis=1)
        total[...] += scatter_columns(value, code, blocks)

    sent = side_by_side(total[...].astype(BF), full)
    for step in range(tiles):
        outs[step][...] = sent[:, step * capp : (step + 1) * capp]


def forward_kernel(place_ref, count_ref, feat_ref, first_ref, second_ref, nb_ref, wf_ref, *refs):
    hidden_ref, gate_ref, picked_ref, blocks_ref = refs
    full, rows = feat_ref.shape
    half = rows // 2
    start, _ = half_of(place_ref[1], rows)
    offsets = nb_ref.shape[0]
    step = 9 if offsets % 9 == 0 else 1
    first, second = first_ref[...], second_ref[...]
    odd = (place_ref[0] & 1) == 1
    below, above = jnp.where(odd, first, second), jnp.where(odd, second, first)
    set_blocks(blocks_ref, jnp.concatenate([feat_ref[...], below, above], axis=1))

    @pl.loop(0, offsets // step)
    def _(group):
        for index in range(step):
            offset = group * step + index
            code = nb_ref[pl.ds(offset, 1), pl.ds(start, half)]
            picked_ref[offset] = gather_columns(blocks_ref[...], code, full)

    pre = jnp.zeros((full, half), F32)
    for offset in range(offsets):
        pre = pre + dot(wf_ref[offset], picked_ref[offset])
    line = start + lax.broadcasted_iota(jnp.int32, (1, half), 1)
    valid = jnp.where(line < count_ref[0], 1.0, 0.0)
    gate_ref[...] = jnp.where(pre > 0, valid, 0.0).astype(BF)
    hidden_ref[...] = (jnp.maximum(pre, 0.0) * valid).astype(BF)


def place_kernel(tiles, capp, place_ref, slots_ref, own_ref, other_ref, *outs):
    full, half = own_ref.shape
    start, other = half_of(place_ref[1], 2 * half)
    hidden = jnp.concatenate([own_ref[...], other_ref[...]], axis=1)
    code = jnp.concatenate(
        [slots_ref[0:1, pl.ds(start, half)], slots_ref[0:1, pl.ds(other, half)]], axis=1
    )
    placed = scatter_columns(hidden, code, tiles * capp // LO).astype(BF)
    outgoing = side_by_side(placed, full)
    for step in range(tiles):
        outs[step][...] = outgoing[:, step * capp : (step + 1) * capp]


def backward_kernel(tiles, cw, *refs):
    (place_ref, slots_ref, gate_ref, picked_ref, wz_ref, nb_ref), refs = refs[:6], refs[6:]
    takes, refs = unpack(refs, tiles)
    terms, other_terms, table_ref, other_table, blocks_ref, grad_ref, total = refs
    chan = place_ref[1]
    full, half = gate_ref.shape
    start, _ = half_of(chan, 2 * half)
    offsets = nb_ref.shape[0]
    padded = wz_ref.shape[1]
    step = 3 if offsets % 3 == 0 else 1
    set_blocks(blocks_ref, jnp.concatenate([take[...] for take in takes], axis=1))
    code = slots_ref[1:2, pl.ds(start, half)]
    grad = gather_columns(blocks_ref[...], code, full) * gate_ref[...]
    grad_ref[...] = grad
    pair_grad = dot(pair_rows(padded, full, cw, chan), grad).astype(BF)
    total[...] = jnp.zeros_like(total)
    for offset in range(offsets, terms.shape[0]):
        terms[offset] = jnp.zeros(terms.shape[1:], F32)
        other_terms[offset] = jnp.zeros(terms.shape[1:], BF)
    count = total.shape[0] // padded

    @pl.loop(0, offsets // step)
    def _(group):
        first = group * step
        line = dot_nt(pair_grad, picked_ref[pl.ds(first, step)].reshape(step * full, half))
        values = dot(wz_ref[pl.ds(first, step)].reshape(step * padded, full), grad_ref[...])
        values = values.astype(BF)
        sums = None
        for index in range(step):
            part = line[:, index * full : (index + 1) * full]
            terms[first + index] = part[:cw]
            other_terms[first + index] = part[cw : 2 * cw].astype(BF)
            code = nb_ref[pl.ds(first + index, 1), pl.ds(start, half)]
            part = scatter_columns(values[index * padded : (index + 1) * padded], code, count)
            sums = part if sums is None else sums + part
        total[...] += sums

    for block in range(count):
        lanes = slice(block * LO, (block + 1) * LO)
        first = block * padded
        table_ref[:, lanes] = total[first : first + cw, :]
        other_table[:, lanes] = total[first + cw : first + 2 * cw, :].astype(BF)


def child_kernel(tiles, cap, capp, ratio, *refs):
    (place_ref, child_ref, cot_ref), refs = refs[:3], refs[3:]
    takes, (picked_ref, terms), refs = unpack(refs, tiles, 2)
    blocks_ref, code_pad, cot_pad = refs
    kids, width = child_ref.shape
    full = picked_ref.shape[1]
    cw = cot_ref.shape[0] // ratio
    cot_pad[...] = jnp.zeros_like(cot_pad)
    cot_pad[:, :width] = cot_ref[...]
    child_codes(code_pad, child_ref[...], place_ref[0], -1, tiles, cap, capp)
    set_blocks(blocks_ref, jnp.concatenate([take[...] for take in takes], axis=1))
    for line in range(kids * ratio, terms.shape[0]):
        terms[line] = jnp.zeros(terms.shape[1:], F32)
    wide = code_pad.shape[1]
    for first in range(0, kids, 2):
        code = jnp.concatenate([code_pad[kid : kid + 1, :] for kid in (first, first + 1)], axis=1)
        both = gather_columns(blocks_ref[...], code, full)
        for kid in (first, first + 1):
            picked = both[:, (kid - first) * wide : (kid - first + 1) * wide]
            picked_ref[kid] = picked
            line = dot_nt(cot_pad[...], picked)
            for piece in range(ratio):
                terms[kid * ratio + piece] = line[piece * cw : (piece + 1) * cw]


def coarse_kernel(place_ref, picked_ref, wc_ref, coarse_ref, total):
    own, width = coarse_ref.shape
    sums = None
    for kid in range(picked_ref.shape[0]):
        part = dot(wc_ref[kid], picked_ref[kid])
        sums = part if sums is None else sums + part
    total[...] = sums
    start = pl.multiple_of(place_ref[1] * own, 8)
    coarse_ref[...] = total[pl.ds(start, own), :][:, :width].astype(BF)


def pack_kernel(tiles, *refs):
    (place_ref, fine_ref, fine_other, table_ref, table_other, terms), refs = refs[:6], refs[6:]
    outs, (own_ref,) = refs[:tiles], refs[tiles:]
    tile = place_ref[0]
    full = fine_ref.shape[2]
    rows = own_ref.shape[1]
    rim = (table_ref.shape[1] - rows) // 2
    fine_part = fine_ref.shape[0] // tiles
    coarse_part = terms.shape[0] // tiles
    used = (fine_part + coarse_part) * full
    base = up_to(used, 128)
    own_ref[...] = table_ref[:, :rows] + table_other[:, :rows].astype(F32)
    for step in range(tiles):
        out = outs[step]
        out[...] = jnp.zeros_like(out)
        peer = lax.rem(tile + step, tiles)
        fine = pl.ds(peer * fine_part, fine_part)
        fines = fine_ref[fine] + fine_other[fine].astype(F32)
        coarses = terms[pl.ds(peer * coarse_part, coarse_part)]
        units = [fines[unit] for unit in range(fine_part)]
        units += [coarses[unit] for unit in range(coarse_part)]
        out[:, :used] = jnp.concatenate(units, axis=1).astype(BF)
        for side in range(2):
            if step == (tiles - 1, 1)[side]:
                lanes = slice(rows + side * rim, rows + (side + 1) * rim)
                out[:, base : base + rim] = (
                    table_ref[:, lanes] + table_other[:, lanes].astype(F32)
                ).astype(BF)


def finish_kernel(place_ref, count_ref, own_ref, halo_ref, up_ref, down_ref, out_ref):
    rows = own_ref.shape[1]
    width = halo_ref.shape[1]
    base = up_ref.shape[1] - width
    tile, last = place_ref[0], place_ref[-1 + place_ref.shape[0]]
    total = own_ref[...]
    for side, take, there in ((1, down_ref, tile < last), (0, up_ref, tile > 0)):
        picks = lax.broadcasted_iota(jnp.int32, (rows, width), 0) == halo_ref[side : side + 1, :]
        hits = jnp.where(picks & there, 1.0, 0.0).astype(BF)
        total = total + dot_nt(take[:, base:], hits)
    out_ref[...] = (total * valid_row(count_ref, rows)).astype(BF)


def sum_kernel(scale, *refs):
    takes, out = refs[:-1], refs[-1]
    width = out.shape[1]
    total = takes[0][:, :width].astype(F32)
    for take in takes[1:]:
        total = total + take[:, :width].astype(F32)
    out[...] = (total * scale).astype(BF)


def collect_kernel(tiles, fine_part, place_ref, *refs):
    takes, (fine_ref, coarse_ref, fines, coarses) = refs[:tiles], refs[tiles:]
    tile = place_ref[0]
    cw, full = fine_ref.shape[1:]
    ratio = coarse_ref.shape[1] // cw
    coarse_part = coarses.shape[0] // tiles
    for step in range(tiles):
        peer = lax.rem(tile + tiles - step, tiles)
        take = takes[step][...].astype(F32)
        units = [
            take[:, unit * full : (unit + 1) * full]
            for unit in range(fine_part + coarse_part * ratio)
        ]
        for line in range(fine_part):
            fines[peer * fine_part + line] = units[line]
        for line in range(coarse_part):
            for piece in range(ratio):
                coarses[peer * coarse_part + line, piece * cw : (piece + 1) * cw, :] = units[
                    fine_part + line * ratio + piece
                ]
    fine_ref[...] = fines[: fine_ref.shape[0]]
    coarse_ref[...] = coarses[: coarse_ref.shape[0]]


def call(body, name, micros, outs, scalars, arrays, scratch=()):
    return pl.pallas_call(
        body,
        out_shape=outs,
        in_specs=[pl.BlockSpec(memory_space=pltpu.SMEM)] * len(scalars)
        + [pl.BlockSpec(memory_space=pltpu.VMEM)] * len(arrays),
        out_specs=jax.tree.map(lambda _: pl.BlockSpec(memory_space=pltpu.VMEM), outs),
        scratch_shapes=scratch,
        name=name,
        cost_estimate=pl.CostEstimate(
            flops=micros * FLOPS_PER_US, bytes_accessed=0, transcendentals=0
        ),
        compiler_params=pltpu.CompilerParams(vmem_limit_bytes=VMEM_LIMIT),
    )(*scalars, *arrays)


def exchange(chunks):
    tiles = len(chunks)
    if tiles <= 4:
        return [chunks[0]] + [
            lax.ppermute(chunks[step], "slab", [(i, (i + step) % tiles) for i in range(tiles)])
            for step in range(1, tiles)
        ]
    tile = lax.axis_index("slab")
    order = jnp.arange(tiles)
    stacked = jnp.take(jnp.stack(chunks), (order - tile) % tiles, axis=0)
    taken = lax.all_to_all(stacked, "slab", split_axis=0, concat_axis=0, tiled=True)
    taken = jnp.take(taken, (tile - order) % tiles, axis=0)
    return [taken[step] for step in range(tiles)]


def other_core(block):
    count = lax.axis_size("chan")
    return lax.ppermute(block, "chan", [(i, i ^ 1) for i in range(count)])


def spread(chunk, tiles):
    return exchange([chunk] * tiles)


def along_x(block):
    count = lax.axis_size("chan")
    moves = [[(i, (i + step) % count) for i in range(count)] for step in range(2, count, 2)]
    return [block] + [lax.ppermute(block, "chan", move) for move in moves]


def names_along(chan, count):
    near = [(chan - step) % count for step in range(0, count, 2)]
    return near + [name ^ 1 for name in near]


def local(
    features, neighbors, halo_rows, counts, owners, children, weight_fine, weight_coarse, cotangent
):
    tiles = lax.axis_size("slab")
    tile, chan = lax.axis_index("slab"), lax.axis_index("chan")
    cw, rows = features.shape
    halo = halo_rows.shape[1]
    own, width = cotangent.shape
    offsets, full = weight_fine.shape[0], weight_fine.shape[2]
    kids, wide = weight_coarse.shape[0], weight_coarse.shape[1]
    cap = 9 * rows // (8 * tiles)
    capp = up_to(cap, 128)
    padded = up_to(2 * cw, 16)
    half = rows // 2
    ext = rows + 2 * halo
    widep = up_to(width, 128)
    blocks = tiles * capp // LO
    ratio = own // cw
    fine_part, coarse_part = -(-offsets // tiles), -(-kids // tiles)
    parts = fine_part + coarse_part * ratio
    base = up_to(parts * full, 128)
    shape = jax.ShapeDtypeStruct

    names = names_along(chan, lax.axis_size("chan"))
    masked = jnp.where(jnp.arange(rows) < counts[0], features, 0).astype(BF)
    edges = jnp.clip(halo_rows, 0, rows - 1)
    far, near = along_x(features)[1:], other_core(features)
    other_cot = other_core(cotangent)
    masked, edges, near, other_cot, *far = lax.optimization_barrier(
        (masked, edges, near, other_cot, *far)
    )
    feats = [masked, *far, near] + [other_core(piece) for piece in far]
    place = jnp.stack([tile, chan, *names, jnp.int32(tiles - 1)]).astype(jnp.int32)
    slots, wz = call(
        functools.partial(select_kernel, tiles, capp, cw),
        "select",
        3,
        [shape((8, rows), jnp.int32), shape((offsets, padded, full), BF)],
        (place,),
        (owners.reshape(1, rows), weight_fine),
    )
    feat, first, second = call(
        functools.partial(gather_kernel, len(feats)),
        "gather",
        2,
        [shape((full, rows), BF)]
        + [shape((full, halo), BF)] * 2,
        (place, counts),
        (edges, *feats),
        [pltpu.VMEM((full, rows), F32)],
    )
    cot, other_cot, first, second = lax.optimization_barrier((cotangent, other_cot, first, second))
    cots = along_x(cot) + along_x(other_cot)
    pairs = edge_pairs(tiles)
    first = lax.ppermute(first, "slab", pairs[0])
    second = lax.ppermute(second, "slab", pairs[1])
    slot_out = call(
        functools.partial(slot_kernel, tiles, cap, capp, len(feats)),
        "slots",
        5,
        [shape((full, capp), BF)] * tiles,
        (place,),
        (children, weight_coarse, *cots),
        [
            pltpu.VMEM((wide, widep), F32),
            pltpu.VMEM((kids, widep), jnp.int32),
            pltpu.VMEM((blocks * full, LO), F32),
        ],
    )
    slot_in = exchange(slot_out)

    hidden, gate, picked = call(
        forward_kernel,
        "forward",
        7,
        [shape((full, half), BF)] * 2 + [shape((offsets, full, half), BF)],
        (place, counts),
        (feat, first, second, neighbors, weight_fine),
        [pltpu.VMEM((ext // LO * full, LO), BF)],
    )
    hidden_out = call(
        functools.partial(place_kernel, tiles, capp),
        "place",
        1,
        [shape((full, capp), BF)] * tiles,
        (place,),
        (slots, hidden, other_core(hidden)),
    )
    hidden_in = exchange(hidden_out)

    fine, other_fine, table, other_table = call(
        functools.partial(backward_kernel, tiles, cw),
        "backward",
        6,
        [
            shape((tiles * fine_part, cw, full), F32),
            shape((tiles * fine_part, cw, full), BF),
            shape((cw, ext), F32),
            shape((cw, ext), BF),
        ],
        (place,),
        (slots, gate, picked, wz, neighbors, *slot_in),
        [
            pltpu.VMEM((blocks * full, LO), BF),
            pltpu.VMEM((full, half), BF),
            pltpu.VMEM((ext // LO * padded, LO), F32),
        ],
    )
    other_fine, other_table = other_core(other_fine), other_core(other_table)

    kept, terms = call(
        functools.partial(child_kernel, tiles, cap, capp, ratio),
        "children",
        4,
        [shape((kids, full, widep), BF), shape((tiles * coarse_part * ratio, cw, full), F32)],
        (place,),
        (children, cotangent, *hidden_in),
        [
            pltpu.VMEM((blocks * full, LO), BF),
            pltpu.VMEM((kids, widep), jnp.int32),
            pltpu.VMEM((own, widep), BF),
        ],
    )
    *part_out, own_grad = call(
        functools.partial(pack_kernel, tiles),
        "pack",
        1,
        [
            shape((cw, base + (halo if tiles > 4 or step in (1, tiles - 1) else 0)), BF)
            for step in range(tiles)
        ]
        + [shape((cw, rows), F32)],
        (place,),
        (fine, other_fine, table, other_table, terms),
    )
    part_in = exchange(part_out)
    coarse = call(
        coarse_kernel,
        "coarse",
        2,
        shape((own, width), BF),
        (place,),
        (kept, weight_coarse),
        [pltpu.VMEM((wide, widep), F32)],
    )

    scale = float(rows * tiles) ** (-0.5)
    part_sum = call(
        functools.partial(sum_kernel, scale), "sums", 1, shape((cw, base), BF), (), part_in
    )
    grad_input = call(
        finish_kernel,
        "finish",
        2,
        shape((cw, rows), BF),
        (place, counts),
        (own_grad, halo_rows, part_in[1], part_in[tiles - 1]),
    )
    grad_fine, grad_coarse = call(
        functools.partial(collect_kernel, tiles, fine_part),
        "collect",
        1,
        [shape((offsets, cw, full), F32), shape((kids, own, full), F32)],
        (place,),
        spread(part_sum, tiles),
        [
            pltpu.VMEM((tiles * fine_part, cw, full), F32),
            pltpu.VMEM((tiles * coarse_part, own, full), F32),
        ],
    )
    return coarse, grad_fine, grad_coarse, grad_input


def solution(mesh):
    return jax.shard_map(
        local,
        mesh=mesh,
        in_specs=(
            P("chan", ("groups", "slab")),
            P(None, ("groups", "slab")),
            P(None, ("groups", "slab")),
            P(("groups", "slab")),
            P(("groups", "slab"), None),
            P(None, ("groups", "slab")),
            P(),
            P(),
            P("chan", ("groups", "slab")),
        ),
        out_specs=(
            P("chan", ("groups", "slab")),
            P("groups", "chan", None),
            P("groups", "chan", None),
            P("chan", ("groups", "slab")),
        ),
        check_vma=False,
    )
```

```python
import functools

import jax
import jax.numpy as jnp
from jax import lax
from jax.experimental import pallas as pl
from jax.experimental.pallas import tpu as pltpu
from jax.sharding import PartitionSpec as P

BF = jnp.bfloat16
F32 = jnp.float32
LO = 256
VMEM_LIMIT = 28 * 1024 * 1024
FLOPS_PER_US = 1_100_000_000


def up_to(value, step):
    return -(-value // step) * step


def dot(left, right):
    return jnp.dot(left, right, preferred_element_type=F32)


def dot_nt(left, right):
    return lax.dot_general(left, right, (((1,), (1,)), ((), ())), preferred_element_type=F32)


def dot_tn(left, right):
    return lax.dot_general(left, right, (((0,), (0,)), ((), ())), preferred_element_type=F32)


def one_hot(code, width=LO):
    low = code & (width - 1)
    rows = lax.broadcasted_iota(jnp.int32, (width, code.shape[1]), 0)
    return jnp.where(rows == low, 1.0, 0.0).astype(BF)


def gather_columns(blocks, code, channels):
    count = blocks.shape[0] // channels
    high = code >> 8
    found = dot(blocks, one_hot(code))
    picked = jnp.zeros((channels, code.shape[1]), F32)
    for block in range(count):
        picked = jnp.where(high == block, found[block * channels : (block + 1) * channels], picked)
    return picked.astype(BF)


def scatter_columns(values, code, count):
    high = code >> 8
    spread = jnp.concatenate(
        [values * jnp.where(high == block, 1.0, 0.0).astype(BF) for block in range(count)], axis=0
    )
    return dot_nt(spread, one_hot(code))


def split_slot(slots, cap, tiles):
    source = jnp.zeros_like(slots)
    for tile in range(1, tiles + 1):
        source = source + jnp.where(slots >= tile * cap, 1, 0)
    return source, slots - source * cap


def edge_pairs(tiles):
    first = [(i, i + 1) for i in range(0, tiles - 1, 2)]
    second = [(i, i + 1) for i in range(1, tiles - 1, 2)]
    return [pairs + [(j, i) for i, j in pairs] for pairs in (first, second)]


def wrapped(value, tiles):
    return jnp.where(value < 0, value + tiles, value)


def pair_rows(lines, full, cw, chan):
    line = lax.broadcasted_iota(jnp.int32, (lines, full), 0)
    column = lax.broadcasted_iota(jnp.int32, (lines, full), 1)
    target = jnp.where(line < cw, chan * cw + line, (chan ^ 1) * cw + line - cw)
    return jnp.where((column == target) & (line < 2 * cw), 1.0, 0.0).astype(BF)


def half_of(chan, rows):
    half = rows // 2
    return pl.multiple_of((chan & 1) * half, half), pl.multiple_of((1 - (chan & 1)) * half, half)


def unpack(refs, *counts):
    groups, start = [], 0
    for count in counts:
        groups.append(refs[start : start + count])
        start += count
    return (*groups, refs[start:])


def valid_row(count_ref, rows):
    return jnp.where(lax.broadcasted_iota(jnp.int32, (1, rows), 1) < count_ref[0], 1.0, 0.0)


def reordered(pieces, names, stack):
    part, width = pieces[0].shape
    size = part * len(pieces)
    column = lax.broadcasted_iota(jnp.int32, (1, size), 1)
    target = column
    for place, (piece, name) in enumerate(zip(pieces, names)):
        stack[place * part : (place + 1) * part, :width] = piece[...].astype(F32)
        inside = (column >= place * part) & (column < (place + 1) * part)
        target = jnp.where(inside, column + (name - place) * part, target)
    order = jnp.where(lax.broadcasted_iota(jnp.int32, (size, size), 0) == target, 1.0, 0.0)
    return dot(order.astype(BF), stack[...].astype(BF)).astype(BF)


def set_blocks(blocks_ref, table):
    channels = table.shape[0]
    for block in range(table.shape[1] // LO):
        blocks_ref[block * channels : (block + 1) * channels, :] = table[
            :, block * LO : (block + 1) * LO
        ]


def padded_table(takes, blocks_ref):
    channels, each = takes[0].shape
    width = blocks_ref.shape[0] // channels * LO
    rest = width - each * len(takes)
    columns = [take[...].astype(F32) for take in takes]
    if rest:
        columns.append(jnp.zeros((channels, rest), F32))
    return jnp.concatenate(columns, axis=1).astype(BF)


def side_by_side(stacked, channels):
    return jnp.concatenate(
        [stacked[start : start + channels] for start in range(0, stacked.shape[0], channels)], axis=1
    )


def child_codes(code_pad, child, tile, sign, tiles, cap, capp):
    source, rank = split_slot(child, cap, tiles)
    code = wrapped(sign * (source - tile), tiles) * capp + rank
    code_pad[...] = jnp.full(code_pad.shape, tiles * capp, jnp.int32)
    code_pad[:, : child.shape[1]] = jnp.where(source == tiles, tiles * capp, code)


def gather_kernel(pieces, *refs):
    (place_ref, count_ref, halo_ref), refs = refs[:3], refs[3:]
    feats, (feat_ref, first_ref, second_ref, feat_stack) = refs[:pieces], refs[pieces:]
    tile = place_ref[0]
    rows = feat_ref.shape[1]
    names = [place_ref[2 + piece] for piece in range(pieces)]
    valid = valid_row(count_ref, rows)
    table = (reordered(feats, names, feat_stack).astype(F32) * valid).astype(BF)
    feat_ref[...] = table
    width = first_ref.shape[1]
    odd = tile & 1
    lower, upper = halo_ref[0:1, :], halo_ref[1:2, :]
    for side, out in ((0, first_ref), (1, second_ref)):
        chosen = jnp.where(odd == side, upper, lower)
        picks = lax.broadcasted_iota(jnp.int32, (rows, width), 0) == chosen
        out[...] = dot(table, jnp.where(picks, 1.0, 0.0).astype(BF)).astype(BF)


def select_kernel(tiles, capp, cw, place_ref, owner_ref, wf_ref, slots_ref, wz_ref):
    tile = place_ref[0]
    owner = owner_ref[...]
    rows = owner.shape[1]
    bins, lanes = up_to(tiles, 16), 128
    same = jnp.where(lax.broadcasted_iota(jnp.int32, (bins, rows), 0) == owner, 1.0, 0.0)
    stacked = jnp.concatenate(
        [same[:, start : start + lanes] for start in range(0, rows, lanes)], axis=0
    )
    first = lax.broadcasted_iota(jnp.int32, (lanes, 2 * lanes), 0)
    second = lax.broadcasted_iota(jnp.int32, (lanes, 2 * lanes), 1)
    before = jnp.where((first < second) | (second >= lanes), 1.0, 0.0).astype(BF)
    earlier = dot(stacked.astype(BF), before)
    above = jnp.zeros((bins, lanes), F32)
    for block in range(rows // lanes):
        start = block * lanes
        lines = slice(block * bins, (block + 1) * bins)
        ranks = (earlier[lines, :lanes] + above) * same[:, start : start + lanes]
        rank = jnp.sum(ranks, axis=0, keepdims=True).astype(jnp.int32)
        above = above + earlier[lines, lanes:]
        name = owner[:, start : start + lanes]
        slots_ref[0:1, start : start + lanes] = wrapped(name - tile, tiles) * capp + rank
        slots_ref[1:2, start : start + lanes] = wrapped(tile - name, tiles) * capp + rank
    own = pair_rows(wz_ref.shape[1], wz_ref.shape[2], cw, place_ref[1])
    for offset in range(wz_ref.shape[0]):
        wz_ref[offset] = dot_nt(own, wf_ref[offset]).astype(BF)


def slot_kernel(tiles, cap, capp, pieces, *refs):
    (place_ref, child_ref, wc_ref), refs = refs[:3], refs[3:]
    cots, outs, (cot_stack, code_pad, total) = unpack(refs, pieces, tiles)
    tile = place_ref[0]
    names = [place_ref[2 + piece] for piece in range(pieces)]
    kids = child_ref.shape[0]
    full = wc_ref.shape[2]
    blocks = total.shape[0] // full
    cot_stack[...] = jnp.zeros_like(cot_stack)
    cot = reordered(cots, names, cot_stack)
    child_codes(code_pad, child_ref[...], tile, 1, tiles, cap, capp)
    total[...] = jnp.zeros_like(total)
    for first in range(0, kids, 2):
        pair = (first, first + 1)
        value = jnp.concatenate([dot_tn(wc_ref[kid], cot).astype(BF) for kid in pair], axis=1)
        code = jnp.concatenate([code_pad[kid : kid + 1, :] for kid in pair], axis=1)
        total[...] += scatter_columns(value, code, blocks)

    sent = side_by_side(total[...].astype(BF), full)
    for step in range(tiles):
        outs[step][...] = sent[:, step * capp : (step + 1) * capp]


def forward_kernel(place_ref, count_ref, feat_ref, first_ref, second_ref, nb_ref, wf_ref, *refs):
    hidden_ref, gate_ref, picked_ref, blocks_ref = refs
    full, rows = feat_ref.shape
    half = rows // 2
    start, _ = half_of(place_ref[1], rows)
    offsets = nb_ref.shape[0]
    step = 9 if offsets % 9 == 0 else 1
    first, second = first_ref[...], second_ref[...]
    odd = (place_ref[0] & 1) == 1
    below, above = jnp.where(odd, first, second), jnp.where(odd, second, first)
    set_blocks(blocks_ref, jnp.concatenate([feat_ref[...], below, above], axis=1))

    @pl.loop(0, offsets // step)
    def _(group):
        for index in range(step):
            offset = group * step + index
            code = nb_ref[pl.ds(offset, 1), pl.ds(start, half)]
            picked_ref[offset] = gather_columns(blocks_ref[...], code, full)

    pre = jnp.zeros((full, half), F32)
    for offset in range(offsets):
        pre = pre + dot(wf_ref[offset], picked_ref[offset])
    line = start + lax.broadcasted_iota(jnp.int32, (1, half), 1)
    valid = jnp.where(line < count_ref[0], 1.0, 0.0)
    gate_ref[...] = jnp.where(pre > 0, valid, 0.0).astype(BF)
    hidden_ref[...] = (jnp.maximum(pre, 0.0) * valid).astype(BF)


def place_kernel(tiles, capp, place_ref, slots_ref, own_ref, other_ref, *outs):
    full, half = own_ref.shape
    start, other = half_of(place_ref[1], 2 * half)
    hidden = jnp.concatenate([own_ref[...], other_ref[...]], axis=1)
    code = jnp.concatenate(
        [slots_ref[0:1, pl.ds(start, half)], slots_ref[0:1, pl.ds(other, half)]], axis=1
    )
    placed = scatter_columns(hidden, code, up_to(tiles * capp, LO) // LO).astype(BF)
    outgoing = side_by_side(placed, full)
    for step in range(tiles):
        outs[step][...] = outgoing[:, step * capp : (step + 1) * capp]


def backward_kernel(tiles, cw, *refs):
    (place_ref, slots_ref, gate_ref, picked_ref, wz_ref, nb_ref), refs = refs[:6], refs[6:]
    takes, refs = unpack(refs, tiles)
    terms, other_terms, table_ref, other_table, blocks_ref, grad_ref, total = refs
    chan = place_ref[1]
    full, half = gate_ref.shape
    start, _ = half_of(chan, 2 * half)
    offsets = nb_ref.shape[0]
    padded = wz_ref.shape[1]
    step = 9 if offsets % 9 == 0 else 1
    set_blocks(blocks_ref, padded_table(takes, blocks_ref))
    code = slots_ref[1:2, pl.ds(start, half)]
    grad = gather_columns(blocks_ref[...], code, full) * gate_ref[...]
    grad_ref[...] = grad
    pair_grad = dot(pair_rows(padded, full, cw, chan), grad).astype(BF)
    total[...] = jnp.zeros_like(total)
    for offset in range(offsets, terms.shape[0]):
        terms[offset] = jnp.zeros(terms.shape[1:], F32)
        other_terms[offset] = jnp.zeros(terms.shape[1:], BF)
    count = total.shape[0] // padded

    @pl.loop(0, offsets // step)
    def _(group):
        first = group * step
        line = dot_nt(pair_grad, picked_ref[pl.ds(first, step)].reshape(step * full, half))
        values = dot(wz_ref[pl.ds(first, step)].reshape(step * padded, full), grad_ref[...])
        values = values.astype(BF)
        sums = None
        for index in range(step):
            part = line[:, index * full : (index + 1) * full]
            terms[first + index] = part[:cw]
            other_terms[first + index] = part[cw : 2 * cw].astype(BF)
            code = nb_ref[pl.ds(first + index, 1), pl.ds(start, half)]
            part = scatter_columns(values[index * padded : (index + 1) * padded], code, count)
            sums = part if sums is None else sums + part
        total[...] += sums

    for block in range(count):
        lanes = slice(block * LO, (block + 1) * LO)
        first = block * padded
        table_ref[:, lanes] = total[first : first + cw, :]
        other_table[:, lanes] = total[first + cw : first + 2 * cw, :].astype(BF)


def child_kernel(tiles, cap, capp, ratio, *refs):
    (place_ref, child_ref, cot_ref), refs = refs[:3], refs[3:]
    takes, (picked_ref, terms), refs = unpack(refs, tiles, 2)
    blocks_ref, code_pad, cot_pad = refs
    kids, width = child_ref.shape
    full = picked_ref.shape[1]
    cw = cot_ref.shape[0] // ratio
    cot_pad[...] = jnp.zeros_like(cot_pad)
    cot_pad[:, :width] = cot_ref[...]
    child_codes(code_pad, child_ref[...], place_ref[0], -1, tiles, cap, capp)
    set_blocks(blocks_ref, padded_table(takes, blocks_ref))
    for line in range(kids * ratio, terms.shape[0]):
        terms[line] = jnp.zeros(terms.shape[1:], F32)
    wide = code_pad.shape[1]
    for first in range(0, kids, 2):
        code = jnp.concatenate([code_pad[kid : kid + 1, :] for kid in (first, first + 1)], axis=1)
        both = gather_columns(blocks_ref[...], code, full)
        for kid in (first, first + 1):
            picked = both[:, (kid - first) * wide : (kid - first + 1) * wide]
            picked_ref[kid] = picked
            line = dot_nt(cot_pad[...], picked)
            for piece in range(ratio):
                terms[kid * ratio + piece] = line[piece * cw : (piece + 1) * cw]


def coarse_kernel(place_ref, picked_ref, wc_ref, coarse_ref, total):
    own, width = coarse_ref.shape
    sums = None
    for kid in range(picked_ref.shape[0]):
        part = dot(wc_ref[kid], picked_ref[kid])
        sums = part if sums is None else sums + part
    total[...] = sums
    start = pl.multiple_of(place_ref[1] * own, 8)
    coarse_ref[...] = total[pl.ds(start, own), :][:, :width].astype(BF)


def pack_kernel(tiles, *refs):
    (place_ref, fine_ref, fine_other, table_ref, table_other, terms), refs = refs[:6], refs[6:]
    outs, (own_ref,) = refs[:tiles], refs[tiles:]
    tile = place_ref[0]
    full = fine_ref.shape[2]
    rows = own_ref.shape[1]
    rim = (table_ref.shape[1] - rows) // 2
    fine_part = fine_ref.shape[0] // tiles
    coarse_part = terms.shape[0] // tiles
    used = (fine_part + coarse_part) * full
    base = up_to(used, 128)
    own_ref[...] = table_ref[:, :rows] + table_other[:, :rows].astype(F32)
    for step in range(tiles):
        out = outs[step]
        out[...] = jnp.zeros_like(out)
        peer = lax.rem(tile + step, tiles)
        fine = pl.ds(peer * fine_part, fine_part)
        fines = fine_ref[fine] + fine_other[fine].astype(F32)
        coarses = terms[pl.ds(peer * coarse_part, coarse_part)]
        units = [fines[unit] for unit in range(fine_part)]
        units += [coarses[unit] for unit in range(coarse_part)]
        out[:, :used] = jnp.concatenate(units, axis=1).astype(BF)
        for side in range(2):
            if step == (tiles - 1, 1)[side]:
                lanes = slice(rows + side * rim, rows + (side + 1) * rim)
                out[:, base : base + rim] = (
                    table_ref[:, lanes] + table_other[:, lanes].astype(F32)
                ).astype(BF)


def finish_kernel(place_ref, count_ref, own_ref, halo_ref, up_ref, down_ref, out_ref):
    rows = own_ref.shape[1]
    width = halo_ref.shape[1]
    base = up_ref.shape[1] - width
    tile, last = place_ref[0], place_ref[-1 + place_ref.shape[0]]
    total = own_ref[...]
    for side, take, there in ((1, down_ref, tile < last), (0, up_ref, tile > 0)):
        picks = lax.broadcasted_iota(jnp.int32, (rows, width), 0) == halo_ref[side : side + 1, :]
        hits = jnp.where(picks & there, 1.0, 0.0).astype(BF)
        total = total + dot_nt(take[:, base:], hits)
    out_ref[...] = (total * valid_row(count_ref, rows)).astype(BF)


def sum_kernel(scale, *refs):
    takes, out = refs[:-1], refs[-1]
    width = out.shape[1]
    total = takes[0][:, :width].astype(F32)
    for take in takes[1:]:
        total = total + take[:, :width].astype(F32)
    out[...] = (total * scale).astype(BF)


def collect_kernel(tiles, fine_part, place_ref, *refs):
    takes, (fine_ref, coarse_ref, fines, coarses) = refs[:tiles], refs[tiles:]
    tile = place_ref[0]
    cw, full = fine_ref.shape[1:]
    ratio = coarse_ref.shape[1] // cw
    coarse_part = coarses.shape[0] // tiles
    for step in range(tiles):
        peer = lax.rem(tile + tiles - step, tiles)
        take = takes[step][...].astype(F32)
        units = [
            take[:, unit * full : (unit + 1) * full]
            for unit in range(fine_part + coarse_part * ratio)
        ]
        for line in range(fine_part):
            fines[peer * fine_part + line] = units[line]
        for line in range(coarse_part):
            for piece in range(ratio):
                coarses[peer * coarse_part + line, piece * cw : (piece + 1) * cw, :] = units[
                    fine_part + line * ratio + piece
                ]
    fine_ref[...] = fines[: fine_ref.shape[0]]
    coarse_ref[...] = coarses[: coarse_ref.shape[0]]


def call(body, name, micros, outs, scalars, arrays, scratch=()):
    return pl.pallas_call(
        body,
        out_shape=outs,
        in_specs=[pl.BlockSpec(memory_space=pltpu.SMEM)] * len(scalars)
        + [pl.BlockSpec(memory_space=pltpu.VMEM)] * len(arrays),
        out_specs=jax.tree.map(lambda _: pl.BlockSpec(memory_space=pltpu.VMEM), outs),
        scratch_shapes=scratch,
        name=name,
        cost_estimate=pl.CostEstimate(
            flops=micros * FLOPS_PER_US, bytes_accessed=0, transcendentals=0
        ),
        compiler_params=pltpu.CompilerParams(vmem_limit_bytes=VMEM_LIMIT),
    )(*scalars, *arrays)


def exchange(chunks):
    tiles = len(chunks)
    if tiles <= 4:
        return [chunks[0]] + [
            lax.ppermute(chunks[step], "slab", [(i, (i + step) % tiles) for i in range(tiles)])
            for step in range(1, tiles)
        ]
    tile = lax.axis_index("slab")
    order = jnp.arange(tiles)
    stacked = jnp.take(jnp.stack(chunks), (order - tile) % tiles, axis=0)
    taken = lax.all_to_all(stacked, "slab", split_axis=0, concat_axis=0, tiled=True)
    taken = jnp.take(taken, (tile - order) % tiles, axis=0)
    return [taken[step] for step in range(tiles)]


def other_core(block):
    count = lax.axis_size("chan")
    return lax.ppermute(block, "chan", [(i, i ^ 1) for i in range(count)])


def spread(chunk, tiles):
    return exchange([chunk] * tiles)


def along_x(block):
    count = lax.axis_size("chan")
    moves = [[(i, (i + step) % count) for i in range(count)] for step in range(2, count, 2)]
    return [block] + [lax.ppermute(block, "chan", move) for move in moves]


def names_along(chan, count):
    near = [(chan - step) % count for step in range(0, count, 2)]
    return near + [name ^ 1 for name in near]


def local(
    features, neighbors, halo_rows, counts, owners, children, weight_fine, weight_coarse, cotangent
):
    tiles = lax.axis_size("slab")
    tile, chan = lax.axis_index("slab"), lax.axis_index("chan")
    cw, rows = features.shape
    halo = halo_rows.shape[1]
    own, width = cotangent.shape
    offsets, full = weight_fine.shape[0], weight_fine.shape[2]
    kids, wide = weight_coarse.shape[0], weight_coarse.shape[1]
    cap = 9 * rows // (8 * tiles)
    capp = cap
    padded = up_to(2 * cw, 16)
    half = rows // 2
    ext = rows + 2 * halo
    widep = up_to(width, 128)
    blocks = up_to(tiles * capp, LO) // LO
    ratio = own // cw
    fine_part, coarse_part = -(-offsets // tiles), -(-kids // tiles)
    parts = fine_part + coarse_part * ratio
    base = up_to(parts * full, 128)
    shape = jax.ShapeDtypeStruct

    names = names_along(chan, lax.axis_size("chan"))
    masked = jnp.where(jnp.arange(rows) < counts[0], features, 0).astype(BF)
    edges = jnp.clip(halo_rows, 0, rows - 1)
    far, near = along_x(features)[1:], other_core(features)
    other_cot = other_core(cotangent)
    masked, edges, near, other_cot, *far = lax.optimization_barrier(
        (masked, edges, near, other_cot, *far)
    )
    feats = [masked, *far, near] + [other_core(piece) for piece in far]
    place = jnp.stack([tile, chan, *names, jnp.int32(tiles - 1)]).astype(jnp.int32)
    slots, wz = call(
        functools.partial(select_kernel, tiles, capp, cw),
        "select",
        3,
        [shape((8, rows), jnp.int32), shape((offsets, padded, full), BF)],
        (place,),
        (owners.reshape(1, rows), weight_fine),
    )
    feat, first, second = call(
        functools.partial(gather_kernel, len(feats)),
        "gather",
        2,
        [shape((full, rows), BF)]
        + [shape((full, halo), BF)] * 2,
        (place, counts),
        (edges, *feats),
        [pltpu.VMEM((full, rows), F32)],
    )
    cot, other_cot, first, second = lax.optimization_barrier((cotangent, other_cot, first, second))
    cots = along_x(cot) + along_x(other_cot)
    pairs = edge_pairs(tiles)
    first = lax.ppermute(first, "slab", pairs[0])
    second = lax.ppermute(second, "slab", pairs[1])
    slot_out = call(
        functools.partial(slot_kernel, tiles, cap, capp, len(feats)),
        "slots",
        5,
        [shape((full, capp), BF)] * tiles,
        (place,),
        (children, weight_coarse, *cots),
        [
            pltpu.VMEM((wide, widep), F32),
            pltpu.VMEM((kids, widep), jnp.int32),
            pltpu.VMEM((blocks * full, LO), F32),
        ],
    )
    slot_in = exchange(slot_out)

    hidden, gate, picked = call(
        forward_kernel,
        "forward",
        7,
        [shape((full, half), BF)] * 2 + [shape((offsets, full, half), BF)],
        (place, counts),
        (feat, first, second, neighbors, weight_fine),
        [pltpu.VMEM((ext // LO * full, LO), BF)],
    )
    hidden_out = call(
        functools.partial(place_kernel, tiles, capp),
        "place",
        1,
        [shape((full, capp), BF)] * tiles,
        (place,),
        (slots, hidden, other_core(hidden)),
    )
    hidden_in = exchange(hidden_out)

    fine, other_fine, table, other_table = call(
        functools.partial(backward_kernel, tiles, cw),
        "backward",
        6,
        [
            shape((tiles * fine_part, cw, full), F32),
            shape((tiles * fine_part, cw, full), BF),
            shape((cw, ext), F32),
            shape((cw, ext), BF),
        ],
        (place,),
        (slots, gate, picked, wz, neighbors, *slot_in),
        [
            pltpu.VMEM((blocks * full, LO), BF),
            pltpu.VMEM((full, half), BF),
            pltpu.VMEM((ext // LO * padded, LO), F32),
        ],
    )
    other_fine, other_table = other_core(other_fine), other_core(other_table)

    kept, terms = call(
        functools.partial(child_kernel, tiles, cap, capp, ratio),
        "children",
        4,
        [shape((kids, full, widep), BF), shape((tiles * coarse_part * ratio, cw, full), F32)],
        (place,),
        (children, cotangent, *hidden_in),
        [
            pltpu.VMEM((blocks * full, LO), BF),
            pltpu.VMEM((kids, widep), jnp.int32),
            pltpu.VMEM((own, widep), BF),
        ],
    )
    *part_out, own_grad = call(
        functools.partial(pack_kernel, tiles),
        "pack",
        1,
        [
            shape((cw, base + (halo if tiles > 4 or step in (1, tiles - 1) else 0)), BF)
            for step in range(tiles)
        ]
        + [shape((cw, rows), F32)],
        (place,),
        (fine, other_fine, table, other_table, terms),
    )
    part_in = exchange(part_out)
    coarse = call(
        coarse_kernel,
        "coarse",
        2,
        shape((own, width), BF),
        (place,),
        (kept, weight_coarse),
        [pltpu.VMEM((wide, widep), F32)],
    )

    scale = float(rows * tiles) ** (-0.5)
    part_sum = call(
        functools.partial(sum_kernel, scale), "sums", 1, shape((cw, base), BF), (), part_in
    )
    grad_input = call(
        finish_kernel,
        "finish",
        2,
        shape((cw, rows), BF),
        (place, counts),
        (own_grad, halo_rows, part_in[1], part_in[tiles - 1]),
    )
    grad_fine, grad_coarse = call(
        functools.partial(collect_kernel, tiles, fine_part),
        "collect",
        1,
        [shape((offsets, cw, full), F32), shape((kids, own, full), F32)],
        (place,),
        spread(part_sum, tiles),
        [
            pltpu.VMEM((tiles * fine_part, cw, full), F32),
            pltpu.VMEM((tiles * coarse_part, own, full), F32),
        ],
    )
    return coarse, grad_fine, grad_coarse, grad_input


def solution(mesh):
    return jax.shard_map(
        local,
        mesh=mesh,
        in_specs=(
            P("chan", ("groups", "slab")),
            P(None, ("groups", "slab")),
            P(None, ("groups", "slab")),
            P(("groups", "slab")),
            P(("groups", "slab"), None),
            P(None, ("groups", "slab")),
            P(),
            P(),
            P("chan", ("groups", "slab")),
        ),
        out_specs=(
            P("chan", ("groups", "slab")),
            P("groups", "chan", None),
            P("groups", "chan", None),
            P("chan", ("groups", "slab")),
        ),
        check_vma=False,
    )
```

```python
import functools

import jax
import jax.numpy as jnp
from jax import lax
from jax.experimental import pallas as pl
from jax.experimental.pallas import tpu as pltpu
from jax.sharding import PartitionSpec as P

BF = jnp.bfloat16
F32 = jnp.float32
LO = 256
VMEM_LIMIT = 28 * 1024 * 1024
FLOPS_PER_US = 1_100_000_000


def up_to(value, step):
    return -(-value // step) * step


def dot(left, right):
    return jnp.dot(left, right, preferred_element_type=F32)


def dot_nt(left, right):
    return lax.dot_general(left, right, (((1,), (1,)), ((), ())), preferred_element_type=F32)


def dot_tn(left, right):
    return lax.dot_general(left, right, (((0,), (0,)), ((), ())), preferred_element_type=F32)


def one_hot(code, width=LO):
    low = code & (width - 1)
    rows = lax.broadcasted_iota(jnp.int32, (width, code.shape[1]), 0)
    return jnp.where(rows == low, 1.0, 0.0).astype(BF)


def gather_columns(blocks, code, channels):
    count = blocks.shape[0] // channels
    high = code >> 8
    found = dot(blocks, one_hot(code))
    picked = jnp.zeros((channels, code.shape[1]), F32)
    for block in range(count):
        picked = jnp.where(high == block, found[block * channels : (block + 1) * channels], picked)
    return picked.astype(BF)


def scatter_columns(values, code, count):
    high = code >> 8
    spread = jnp.concatenate(
        [values * jnp.where(high == block, 1.0, 0.0).astype(BF) for block in range(count)], axis=0
    )
    return dot_nt(spread, one_hot(code))


def split_slot(slots, cap, tiles):
    source = jnp.zeros_like(slots)
    for tile in range(1, tiles + 1):
        source = source + jnp.where(slots >= tile * cap, 1, 0)
    return source, slots - source * cap


def edge_pairs(tiles):
    first = [(i, i + 1) for i in range(0, tiles - 1, 2)]
    second = [(i, i + 1) for i in range(1, tiles - 1, 2)]
    return [pairs + [(j, i) for i, j in pairs] for pairs in (first, second)]


def wrapped(value, tiles):
    return jnp.where(value < 0, value + tiles, value)


def pair_rows(lines, full, cw, chan):
    line = lax.broadcasted_iota(jnp.int32, (lines, full), 0)
    column = lax.broadcasted_iota(jnp.int32, (lines, full), 1)
    target = jnp.where(line < cw, chan * cw + line, (chan ^ 1) * cw + line - cw)
    return jnp.where((column == target) & (line < 2 * cw), 1.0, 0.0).astype(BF)


def half_of(chan, rows):
    half = rows // 2
    return pl.multiple_of((chan & 1) * half, half), pl.multiple_of((1 - (chan & 1)) * half, half)


def unpack(refs, *counts):
    groups, start = [], 0
    for count in counts:
        groups.append(refs[start : start + count])
        start += count
    return (*groups, refs[start:])


def valid_row(count_ref, rows):
    return jnp.where(lax.broadcasted_iota(jnp.int32, (1, rows), 1) < count_ref[0], 1.0, 0.0)


def reordered(pieces, names, stack):
    part, width = pieces[0].shape
    size = part * len(pieces)
    column = lax.broadcasted_iota(jnp.int32, (1, size), 1)
    target = column
    for place, (piece, name) in enumerate(zip(pieces, names)):
        stack[place * part : (place + 1) * part, :width] = piece[...].astype(F32)
        inside = (column >= place * part) & (column < (place + 1) * part)
        target = jnp.where(inside, column + (name - place) * part, target)
    order = jnp.where(lax.broadcasted_iota(jnp.int32, (size, size), 0) == target, 1.0, 0.0)
    return dot(order.astype(BF), stack[...].astype(BF)).astype(BF)


def set_blocks(blocks_ref, table):
    channels = table.shape[0]
    for block in range(table.shape[1] // LO):
        blocks_ref[block * channels : (block + 1) * channels, :] = table[
            :, block * LO : (block + 1) * LO
        ]


def padded_table(takes, blocks_ref):
    channels, each = takes[0].shape
    width = blocks_ref.shape[0] // channels * LO
    rest = width - each * len(takes)
    columns = [take[...].astype(F32) for take in takes]
    if rest:
        columns.append(jnp.zeros((channels, rest), F32))
    return jnp.concatenate(columns, axis=1).astype(BF)


def side_by_side(stacked, channels):
    return jnp.concatenate(
        [stacked[start : start + channels] for start in range(0, stacked.shape[0], channels)], axis=1
    )


def child_codes(code_pad, child, tile, sign, tiles, cap, capp):
    source, rank = split_slot(child, cap, tiles)
    code = wrapped(sign * (source - tile), tiles) * capp + rank
    code_pad[...] = jnp.full(code_pad.shape, tiles * capp, jnp.int32)
    code_pad[:, : child.shape[1]] = jnp.where(source == tiles, tiles * capp, code)


def gather_kernel(pieces, *refs):
    (place_ref, count_ref, halo_ref), refs = refs[:3], refs[3:]
    feats, (feat_ref, first_ref, second_ref, feat_stack) = refs[:pieces], refs[pieces:]
    tile = place_ref[0]
    rows = feat_ref.shape[1]
    names = [place_ref[2 + piece] for piece in range(pieces)]
    valid = valid_row(count_ref, rows)
    table = (reordered(feats, names, feat_stack).astype(F32) * valid).astype(BF)
    feat_ref[...] = table
    width = first_ref.shape[1]
    odd = tile & 1
    lower, upper = halo_ref[0:1, :], halo_ref[1:2, :]
    for side, out in ((0, first_ref), (1, second_ref)):
        chosen = jnp.where(odd == side, upper, lower)
        picks = lax.broadcasted_iota(jnp.int32, (rows, width), 0) == chosen
        out[...] = dot(table, jnp.where(picks, 1.0, 0.0).astype(BF)).astype(BF)


def select_kernel(tiles, capp, cw, place_ref, owner_ref, wf_ref, slots_ref, wz_ref):
    tile = place_ref[0]
    owner = owner_ref[...]
    rows = owner.shape[1]
    bins, lanes = up_to(tiles, 16), 128
    same = jnp.where(lax.broadcasted_iota(jnp.int32, (bins, rows), 0) == owner, 1.0, 0.0)
    stacked = jnp.concatenate(
        [same[:, start : start + lanes] for start in range(0, rows, lanes)], axis=0
    )
    first = lax.broadcasted_iota(jnp.int32, (lanes, 2 * lanes), 0)
    second = lax.broadcasted_iota(jnp.int32, (lanes, 2 * lanes), 1)
    before = jnp.where((first < second) | (second >= lanes), 1.0, 0.0).astype(BF)
    earlier = dot(stacked.astype(BF), before)
    above = jnp.zeros((bins, lanes), F32)
    for block in range(rows // lanes):
        start = block * lanes
        lines = slice(block * bins, (block + 1) * bins)
        ranks = (earlier[lines, :lanes] + above) * same[:, start : start + lanes]
        rank = jnp.sum(ranks, axis=0, keepdims=True).astype(jnp.int32)
        above = above + earlier[lines, lanes:]
        name = owner[:, start : start + lanes]
        slots_ref[0:1, start : start + lanes] = wrapped(name - tile, tiles) * capp + rank
        slots_ref[1:2, start : start + lanes] = wrapped(tile - name, tiles) * capp + rank
    own = pair_rows(wz_ref.shape[1], wz_ref.shape[2], cw, place_ref[1])
    for offset in range(wz_ref.shape[0]):
        wz_ref[offset] = dot_nt(own, wf_ref[offset]).astype(BF)


def slot_kernel(tiles, cap, capp, pieces, *refs):
    (place_ref, child_ref, wc_ref), refs = refs[:3], refs[3:]
    cots, outs, (cot_stack, code_pad, total) = unpack(refs, pieces, tiles)
    tile = place_ref[0]
    names = [place_ref[2 + piece] for piece in range(pieces)]
    kids = child_ref.shape[0]
    full = wc_ref.shape[2]
    blocks = total.shape[0] // full
    cot_stack[...] = jnp.zeros_like(cot_stack)
    cot = reordered(cots, names, cot_stack)
    child_codes(code_pad, child_ref[...], tile, 1, tiles, cap, capp)
    total[...] = jnp.zeros_like(total)
    for first in range(0, kids, 2):
        pair = (first, first + 1)
        value = jnp.concatenate([dot_tn(wc_ref[kid], cot).astype(BF) for kid in pair], axis=1)
        code = jnp.concatenate([code_pad[kid : kid + 1, :] for kid in pair], axis=1)
        total[...] += scatter_columns(value, code, blocks)

    sent = side_by_side(total[...].astype(BF), full)
    for step in range(tiles):
        outs[step][...] = sent[:, step * capp : (step + 1) * capp]


def forward_kernel(place_ref, count_ref, feat_ref, first_ref, second_ref, nb_ref, wf_ref, *refs):
    hidden_ref, gate_ref, picked_ref, blocks_ref = refs
    full, rows = feat_ref.shape
    half = rows // 2
    start, _ = half_of(place_ref[1], rows)
    offsets = nb_ref.shape[0]
    step = 27 if offsets % 27 == 0 else 1
    first, second = first_ref[...], second_ref[...]
    odd = (place_ref[0] & 1) == 1
    below, above = jnp.where(odd, first, second), jnp.where(odd, second, first)
    set_blocks(blocks_ref, jnp.concatenate([feat_ref[...], below, above], axis=1))

    @pl.loop(0, offsets // step)
    def _(group):
        for index in range(step):
            offset = group * step + index
            code = nb_ref[pl.ds(offset, 1), pl.ds(start, half)]
            picked_ref[offset] = gather_columns(blocks_ref[...], code, full)

    pre = jnp.zeros((full, half), F32)
    for offset in range(offsets):
        pre = pre + dot(wf_ref[offset], picked_ref[offset])
    line = start + lax.broadcasted_iota(jnp.int32, (1, half), 1)
    valid = jnp.where(line < count_ref[0], 1.0, 0.0)
    gate_ref[...] = jnp.where(pre > 0, valid, 0.0).astype(BF)
    hidden_ref[...] = (jnp.maximum(pre, 0.0) * valid).astype(BF)


def place_kernel(tiles, capp, place_ref, slots_ref, own_ref, other_ref, *outs):
    full, half = own_ref.shape
    start, other = half_of(place_ref[1], 2 * half)
    hidden = jnp.concatenate([own_ref[...], other_ref[...]], axis=1)
    code = jnp.concatenate(
        [slots_ref[0:1, pl.ds(start, half)], slots_ref[0:1, pl.ds(other, half)]], axis=1
    )
    placed = scatter_columns(hidden, code, up_to(tiles * capp, LO) // LO).astype(BF)
    outgoing = side_by_side(placed, full)
    for step in range(tiles):
        outs[step][...] = outgoing[:, step * capp : (step + 1) * capp]


def backward_kernel(tiles, cw, *refs):
    (place_ref, slots_ref, gate_ref, picked_ref, wz_ref, nb_ref), refs = refs[:6], refs[6:]
    takes, refs = unpack(refs, tiles)
    terms, other_terms, table_ref, other_table, blocks_ref, grad_ref, total = refs
    chan = place_ref[1]
    full, half = gate_ref.shape
    start, _ = half_of(chan, 2 * half)
    offsets = nb_ref.shape[0]
    padded = wz_ref.shape[1]
    step = 27 if offsets % 27 == 0 else 1
    set_blocks(blocks_ref, padded_table(takes, blocks_ref))
    code = slots_ref[1:2, pl.ds(start, half)]
    grad = gather_columns(blocks_ref[...], code, full) * gate_ref[...]
    grad_ref[...] = grad
    pair_grad = dot(pair_rows(padded, full, cw, chan), grad).astype(BF)
    total[...] = jnp.zeros_like(total)
    for offset in range(offsets, terms.shape[0]):
        terms[offset] = jnp.zeros(terms.shape[1:], F32)
        other_terms[offset] = jnp.zeros(terms.shape[1:], BF)
    count = total.shape[0] // padded

    @pl.loop(0, offsets // step)
    def _(group):
        first = group * step
        line = dot_nt(pair_grad, picked_ref[pl.ds(first, step)].reshape(step * full, half))
        values = dot(wz_ref[pl.ds(first, step)].reshape(step * padded, full), grad_ref[...])
        values = values.astype(BF)
        sums = None
        for index in range(step):
            part = line[:, index * full : (index + 1) * full]
            terms[first + index] = part[:cw]
            other_terms[first + index] = part[cw : 2 * cw].astype(BF)
            code = nb_ref[pl.ds(first + index, 1), pl.ds(start, half)]
            part = scatter_columns(values[index * padded : (index + 1) * padded], code, count)
            sums = part if sums is None else sums + part
        total[...] += sums

    for block in range(count):
        lanes = slice(block * LO, (block + 1) * LO)
        first = block * padded
        table_ref[:, lanes] = total[first : first + cw, :]
        other_table[:, lanes] = total[first + cw : first + 2 * cw, :].astype(BF)


def child_kernel(tiles, cap, capp, ratio, *refs):
    (place_ref, child_ref, cot_ref), refs = refs[:3], refs[3:]
    takes, (picked_ref, terms), refs = unpack(refs, tiles, 2)
    blocks_ref, code_pad, cot_pad = refs
    kids, width = child_ref.shape
    full = picked_ref.shape[1]
    cw = cot_ref.shape[0] // ratio
    cot_pad[...] = jnp.zeros_like(cot_pad)
    cot_pad[:, :width] = cot_ref[...]
    child_codes(code_pad, child_ref[...], place_ref[0], -1, tiles, cap, capp)
    set_blocks(blocks_ref, padded_table(takes, blocks_ref))
    for line in range(kids * ratio, terms.shape[0]):
        terms[line] = jnp.zeros(terms.shape[1:], F32)
    wide = code_pad.shape[1]
    for first in range(0, kids, 2):
        code = jnp.concatenate([code_pad[kid : kid + 1, :] for kid in (first, first + 1)], axis=1)
        both = gather_columns(blocks_ref[...], code, full)
        for kid in (first, first + 1):
            picked = both[:, (kid - first) * wide : (kid - first + 1) * wide]
            picked_ref[kid] = picked
            line = dot_nt(cot_pad[...], picked)
            for piece in range(ratio):
                terms[kid * ratio + piece] = line[piece * cw : (piece + 1) * cw]


def coarse_kernel(place_ref, picked_ref, wc_ref, coarse_ref, total):
    own, width = coarse_ref.shape
    sums = None
    for kid in range(picked_ref.shape[0]):
        part = dot(wc_ref[kid], picked_ref[kid])
        sums = part if sums is None else sums + part
    total[...] = sums
    start = pl.multiple_of(place_ref[1] * own, 8)
    coarse_ref[...] = total[pl.ds(start, own), :][:, :width].astype(BF)


def pack_kernel(tiles, *refs):
    (place_ref, fine_ref, fine_other, table_ref, table_other, terms), refs = refs[:6], refs[6:]
    outs, (own_ref,) = refs[:tiles], refs[tiles:]
    tile = place_ref[0]
    full = fine_ref.shape[2]
    rows = own_ref.shape[1]
    rim = (table_ref.shape[1] - rows) // 2
    fine_part = fine_ref.shape[0] // tiles
    coarse_part = terms.shape[0] // tiles
    used = (fine_part + coarse_part) * full
    base = up_to(used, 128)
    own_ref[...] = table_ref[:, :rows] + table_other[:, :rows].astype(F32)
    for step in range(tiles):
        out = outs[step]
        out[...] = jnp.zeros_like(out)
        peer = lax.rem(tile + step, tiles)
        fine = pl.ds(peer * fine_part, fine_part)
        fines = fine_ref[fine] + fine_other[fine].astype(F32)
        coarses = terms[pl.ds(peer * coarse_part, coarse_part)]
        units = [fines[unit] for unit in range(fine_part)]
        units += [coarses[unit] for unit in range(coarse_part)]
        out[:, :used] = jnp.concatenate(units, axis=1).astype(BF)
        for side in range(2):
            if step == (tiles - 1, 1)[side]:
                lanes = slice(rows + side * rim, rows + (side + 1) * rim)
                out[:, base : base + rim] = (
                    table_ref[:, lanes] + table_other[:, lanes].astype(F32)
                ).astype(BF)


def finish_kernel(place_ref, count_ref, own_ref, halo_ref, up_ref, down_ref, out_ref):
    rows = own_ref.shape[1]
    width = halo_ref.shape[1]
    base = up_ref.shape[1] - width
    tile, last = place_ref[0], place_ref[-1 + place_ref.shape[0]]
    total = own_ref[...]
    for side, take, there in ((1, down_ref, tile < last), (0, up_ref, tile > 0)):
        picks = lax.broadcasted_iota(jnp.int32, (rows, width), 0) == halo_ref[side : side + 1, :]
        hits = jnp.where(picks & there, 1.0, 0.0).astype(BF)
        total = total + dot_nt(take[:, base:], hits)
    out_ref[...] = (total * valid_row(count_ref, rows)).astype(BF)


def sum_kernel(scale, *refs):
    takes, out = refs[:-1], refs[-1]
    width = out.shape[1]
    total = takes[0][:, :width].astype(F32)
    for take in takes[1:]:
        total = total + take[:, :width].astype(F32)
    out[...] = (total * scale).astype(BF)


def collect_kernel(tiles, fine_part, place_ref, *refs):
    takes, (fine_ref, coarse_ref, fines, coarses) = refs[:tiles], refs[tiles:]
    tile = place_ref[0]
    cw, full = fine_ref.shape[1:]
    ratio = coarse_ref.shape[1] // cw
    coarse_part = coarses.shape[0] // tiles
    for step in range(tiles):
        peer = lax.rem(tile + tiles - step, tiles)
        take = takes[step][...].astype(F32)
        units = [
            take[:, unit * full : (unit + 1) * full]
            for unit in range(fine_part + coarse_part * ratio)
        ]
        for line in range(fine_part):
            fines[peer * fine_part + line] = units[line]
        for line in range(coarse_part):
            for piece in range(ratio):
                coarses[peer * coarse_part + line, piece * cw : (piece + 1) * cw, :] = units[
                    fine_part + line * ratio + piece
                ]
    fine_ref[...] = fines[: fine_ref.shape[0]]
    coarse_ref[...] = coarses[: coarse_ref.shape[0]]


def call(body, name, micros, outs, scalars, arrays, scratch=()):
    return pl.pallas_call(
        body,
        out_shape=outs,
        in_specs=[pl.BlockSpec(memory_space=pltpu.SMEM)] * len(scalars)
        + [pl.BlockSpec(memory_space=pltpu.VMEM)] * len(arrays),
        out_specs=jax.tree.map(lambda _: pl.BlockSpec(memory_space=pltpu.VMEM), outs),
        scratch_shapes=scratch,
        name=name,
        cost_estimate=pl.CostEstimate(
            flops=micros * FLOPS_PER_US, bytes_accessed=0, transcendentals=0
        ),
        compiler_params=pltpu.CompilerParams(vmem_limit_bytes=VMEM_LIMIT),
    )(*scalars, *arrays)


def exchange(chunks):
    tiles = len(chunks)
    if tiles <= 4:
        return [chunks[0]] + [
            lax.ppermute(chunks[step], "slab", [(i, (i + step) % tiles) for i in range(tiles)])
            for step in range(1, tiles)
        ]
    tile = lax.axis_index("slab")
    order = jnp.arange(tiles)
    stacked = jnp.take(jnp.stack(chunks), (order - tile) % tiles, axis=0)
    taken = lax.all_to_all(stacked, "slab", split_axis=0, concat_axis=0, tiled=True)
    taken = jnp.take(taken, (tile - order) % tiles, axis=0)
    return [taken[step] for step in range(tiles)]


def other_core(block):
    count = lax.axis_size("chan")
    return lax.ppermute(block, "chan", [(i, i ^ 1) for i in range(count)])


def spread(chunk, tiles):
    return exchange([chunk] * tiles)


def along_x(block):
    count = lax.axis_size("chan")
    moves = [[(i, (i + step) % count) for i in range(count)] for step in range(2, count, 2)]
    return [block] + [lax.ppermute(block, "chan", move) for move in moves]


def names_along(chan, count):
    near = [(chan - step) % count for step in range(0, count, 2)]
    return near + [name ^ 1 for name in near]


def local(
    features, neighbors, halo_rows, counts, owners, children, weight_fine, weight_coarse, cotangent
):
    tiles = lax.axis_size("slab")
    tile, chan = lax.axis_index("slab"), lax.axis_index("chan")
    cw, rows = features.shape
    halo = halo_rows.shape[1]
    own, width = cotangent.shape
    offsets, full = weight_fine.shape[0], weight_fine.shape[2]
    kids, wide = weight_coarse.shape[0], weight_coarse.shape[1]
    cap = 9 * rows // (8 * tiles)
    capp = cap
    padded = up_to(2 * cw, 16)
    half = rows // 2
    ext = rows + 2 * halo
    widep = up_to(width, 128)
    blocks = up_to(tiles * capp, LO) // LO
    ratio = own // cw
    fine_part, coarse_part = -(-offsets // tiles), -(-kids // tiles)
    parts = fine_part + coarse_part * ratio
    base = up_to(parts * full, 128)
    shape = jax.ShapeDtypeStruct

    names = names_along(chan, lax.axis_size("chan"))
    masked = jnp.where(jnp.arange(rows) < counts[0], features, 0).astype(BF)
    edges = jnp.clip(halo_rows, 0, rows - 1)
    far, near = along_x(features)[1:], other_core(features)
    other_cot = other_core(cotangent)
    masked, edges, near, other_cot, *far = lax.optimization_barrier(
        (masked, edges, near, other_cot, *far)
    )
    feats = [masked, *far, near] + [other_core(piece) for piece in far]
    place = jnp.stack([tile, chan, *names, jnp.int32(tiles - 1)]).astype(jnp.int32)
    slots, wz = call(
        functools.partial(select_kernel, tiles, capp, cw),
        "select",
        3,
        [shape((8, rows), jnp.int32), shape((offsets, padded, full), BF)],
        (place,),
        (owners.reshape(1, rows), weight_fine),
    )
    feat, first, second = call(
        functools.partial(gather_kernel, len(feats)),
        "gather",
        2,
        [shape((full, rows), BF)]
        + [shape((full, halo), BF)] * 2,
        (place, counts),
        (edges, *feats),
        [pltpu.VMEM((full, rows), F32)],
    )
    cot, other_cot, first, second = lax.optimization_barrier((cotangent, other_cot, first, second))
    cots = along_x(cot) + along_x(other_cot)
    pairs = edge_pairs(tiles)
    first = lax.ppermute(first, "slab", pairs[0])
    second = lax.ppermute(second, "slab", pairs[1])
    slot_out = call(
        functools.partial(slot_kernel, tiles, cap, capp, len(feats)),
        "slots",
        5,
        [shape((full, capp), BF)] * tiles,
        (place,),
        (children, weight_coarse, *cots),
        [
            pltpu.VMEM((wide, widep), F32),
            pltpu.VMEM((kids, widep), jnp.int32),
            pltpu.VMEM((blocks * full, LO), F32),
        ],
    )
    slot_in = exchange(slot_out)

    hidden, gate, picked = call(
        forward_kernel,
        "forward",
        7,
        [shape((full, half), BF)] * 2 + [shape((offsets, full, half), BF)],
        (place, counts),
        (feat, first, second, neighbors, weight_fine),
        [pltpu.VMEM((ext // LO * full, LO), BF)],
    )
    hidden_out = call(
        functools.partial(place_kernel, tiles, capp),
        "place",
        1,
        [shape((full, capp), BF)] * tiles,
        (place,),
        (slots, hidden, other_core(hidden)),
    )
    hidden_in = exchange(hidden_out)

    fine, other_fine, table, other_table = call(
        functools.partial(backward_kernel, tiles, cw),
        "backward",
        6,
        [
            shape((tiles * fine_part, cw, full), F32),
            shape((tiles * fine_part, cw, full), BF),
            shape((cw, ext), F32),
            shape((cw, ext), BF),
        ],
        (place,),
        (slots, gate, picked, wz, neighbors, *slot_in),
        [
            pltpu.VMEM((blocks * full, LO), BF),
            pltpu.VMEM((full, half), BF),
            pltpu.VMEM((ext // LO * padded, LO), F32),
        ],
    )
    other_fine, other_table = other_core(other_fine), other_core(other_table)

    kept, terms = call(
        functools.partial(child_kernel, tiles, cap, capp, ratio),
        "children",
        4,
        [shape((kids, full, widep), BF), shape((tiles * coarse_part * ratio, cw, full), F32)],
        (place,),
        (children, cotangent, *hidden_in),
        [
            pltpu.VMEM((blocks * full, LO), BF),
            pltpu.VMEM((kids, widep), jnp.int32),
            pltpu.VMEM((own, widep), BF),
        ],
    )
    *part_out, own_grad = call(
        functools.partial(pack_kernel, tiles),
        "pack",
        1,
        [
            shape((cw, base + (halo if tiles > 4 or step in (1, tiles - 1) else 0)), BF)
            for step in range(tiles)
        ]
        + [shape((cw, rows), F32)],
        (place,),
        (fine, other_fine, table, other_table, terms),
    )
    part_in = exchange(part_out)
    coarse = call(
        coarse_kernel,
        "coarse",
        2,
        shape((own, width), BF),
        (place,),
        (kept, weight_coarse),
        [pltpu.VMEM((wide, widep), F32)],
    )

    scale = float(rows * tiles) ** (-0.5)
    part_sum = call(
        functools.partial(sum_kernel, scale), "sums", 1, shape((cw, base), BF), (), part_in
    )
    grad_input = call(
        finish_kernel,
        "finish",
        2,
        shape((cw, rows), BF),
        (place, counts),
        (own_grad, halo_rows, part_in[1], part_in[tiles - 1]),
    )
    grad_fine, grad_coarse = call(
        functools.partial(collect_kernel, tiles, fine_part),
        "collect",
        1,
        [shape((offsets, cw, full), F32), shape((kids, own, full), F32)],
        (place,),
        spread(part_sum, tiles),
        [
            pltpu.VMEM((tiles * fine_part, cw, full), F32),
            pltpu.VMEM((tiles * coarse_part, own, full), F32),
        ],
    )
    return coarse, grad_fine, grad_coarse, grad_input


def solution(mesh):
    return jax.shard_map(
        local,
        mesh=mesh,
        in_specs=(
            P("chan", ("groups", "slab")),
            P(None, ("groups", "slab")),
            P(None, ("groups", "slab")),
            P(("groups", "slab")),
            P(("groups", "slab"), None),
            P(None, ("groups", "slab")),
            P(),
            P(),
            P("chan", ("groups", "slab")),
        ),
        out_specs=(
            P("chan", ("groups", "slab")),
            P("groups", "chan", None),
            P("groups", "chan", None),
            P("chan", ("groups", "slab")),
        ),
        check_vma=False,
    )
```
